512 devices in a mesh: cand: 64 (over y, z), tp: 8 (over x, core).
Axes of the slice: x: 4, y: 8, z: 8, core: 2. Of those that a mesh axis runs over, the one named last changes fastest.
Arguments:
- hidden_in: bfloat16 [24576, 4096], P('cand', 'tp'), may hold values from -6 to 6
- norm_gain: float32 [4096], replicated, may hold values from 0.1 to 1.9
- w_query: bfloat16 [4096, 4096], P('cand', 'tp'), may hold values from -0.09375 to 0.09375
- w_key: bfloat16 [4096, 1024], P('cand', 'tp'), may hold values from -0.09375 to 0.09375
- w_value: bfloat16 [4096, 1024], P('cand', 'tp'), may hold values from -0.09375 to 0.09375
- q_gain: float32 [128], replicated, may hold values from 0.1 to 1.9
- k_gain: float32 [128], replicated, may hold values from 0.1 to 1.9
- w_out: bfloat16 [4096, 4096], P('tp', 'cand'), may hold values from -0.25 to 0.25
- lengths: int32 [256], P('cand'), may hold values from 48 to 96, as said below
- positions: int32 [256], P('cand'), may hold values from 24 to 95, as said below
Outputs:
- attn_out: bfloat16 [24576, 4096], P('cand', 'tp')
The draws below stay inside these ranges and needn't reach their ends.
Inputs may be any that keep to these rules, and one draw needn't show every extreme that they name: Every candidate has lengths at least 48 and at most 96, and the first candidate of every block of 4 has length 96. `positions`: each interaction slot lies inside its candidate's valid tokens, in its second half.
All inputs are finite; a program needn't handle non-finite values.
Results may differ from the reference program's by a relative error of at most 0.017.
Values may be sent and summed in bfloat16 or wider, within the bound.
A program may use at most 64 MiB of HBM per device.

```python
import jax
import jax.numpy as jnp
from jax import lax

D = 4096
HEADS = 32
KV_HEADS = 8
HD = 128
SEQ = 96
CAND_DEV = 4
NCAND = 256
ROWS = 24576
N_TP = 8


def shared_lengths(key):
    length_key = jax.random.fold_in(key, 11)
    raw = jax.random.randint(length_key, (NCAND,), SEQ // 2, SEQ + 1)
    first = jnp.arange(NCAND) % CAND_DEV == 0
    return jnp.where(first, SEQ, raw).astype(jnp.int32)


def draw_lengths(key, part):
    return shared_lengths(key)


def draw_positions(key, part):
    lengths = shared_lengths(key)
    key = jax.random.fold_in(key, 5)
    raw = jax.random.randint(key, (NCAND,), lengths // 2, lengths)
    first = jnp.arange(NCAND) % CAND_DEV == 0
    return jnp.where(first, SEQ - 1, raw).astype(jnp.int32)


def block_levels(own_key, dims, shards, low, high):
    gain = 1.0
    for axis_at, parts in shards:
        heights = jax.random.uniform(jax.random.fold_in(jax.random.fold_in(own_key, 6), axis_at), (parts,), jnp.float32, low / len(shards), high / len(shards))
        gain = gain * jnp.repeat(jnp.exp(heights), dims[axis_at] // parts).reshape((-1,) + (1,) * (len(dims) - 1 - axis_at))
    return gain


def normal_values(stream_key, extent, scale, most, split=(), kind=jnp.bfloat16):
    factor_of = block_levels(stream_key, extent, split, -0.22, 0.18) if split else 1.0
    entries = jax.random.normal(stream_key, extent, jnp.float32) * scale * factor_of
    return jnp.minimum(jnp.maximum(entries, -most), most).astype(kind)


def setup_inputs(seed: int = 0) -> dict:
    seeds = jax.random.split(jax.random.key(seed), 11)
    return {
        "hidden_in": normal_values(seeds[0], (ROWS, D), 1.0, 6.0, ((0, 64), (1, 8))),
        "norm_gain": jnp.clip(1.0 + 0.18 * jax.random.normal(seeds[1], (D,), jnp.float32), 0.1, 1.9),
        "w_query": normal_values(seeds[2], (D, HEADS * HD), D ** -0.5, 0.09375, ((0, 64), (1, 8))),
        "w_key": normal_values(seeds[3], (D, KV_HEADS * HD), D ** -0.5, 0.09375, ((0, 64), (1, 8))),
        "w_value": normal_values(seeds[4], (D, KV_HEADS * HD), D ** -0.5, 0.09375, ((0, 64), (1, 8))),
        "q_gain": jnp.clip(1.0 + 0.18 * jax.random.normal(seeds[5], (HD,), jnp.float32), 0.1, 1.9),
        "k_gain": jnp.clip(1.0 + 0.18 * jax.random.normal(seeds[6], (HD,), jnp.float32), 0.1, 1.9),
        "w_out": normal_values(seeds[7], (HEADS * HD, D), 512 ** -0.5, 0.25, ((0, 8), (1, 64))),
        "lengths": draw_lengths(jax.random.fold_in(seeds[10], 71), 0),
        "positions": draw_positions(jax.random.fold_in(seeds[10], 71), 0),
    }


EPSILON = 1e-06
THETA = 1000000.0

def head_norm(values, weight):
    return values * lax.rsqrt(lax.optimization_barrier(jnp.mean(values * values, axis=-1, keepdims=True)) + EPSILON) * weight

def rotate(values, cosine, sine):
    half_width = values.shape[-1] // 2
    turned = jnp.concatenate([-values[..., half_width:], values[..., :half_width]], axis=-1)
    return values * cosine + turned * sine

def rope_tables(length, width):
    half_width = width // 2
    frequency = THETA ** (-(jnp.arange(half_width, dtype=jnp.float32) * 2.0 / width))
    angles = jnp.arange(length, dtype=jnp.float32)[:, None] * frequency[None, :]
    angles = jnp.concatenate([angles, angles], axis=-1)
    return (jnp.cos(angles), jnp.sin(angles))

def attend(query, keys, vals, lengths, positions, key_all, value_all, own_index):
    length = query.shape[1]
    scale = float(query.shape[-1]) ** (-0.5)
    scores = jnp.einsum('csngd,ctnd->cngst', query.astype(jnp.float32), keys.astype(jnp.float32)) * scale
    slots = jnp.arange(length)
    causal = slots[None, :] <= slots[:, None]
    valid = slots[None, :] < lengths[:, None]
    allowed = causal[None, None, None, :, :] & valid[:, None, None, None, :]
    weights_local = jnp.where(allowed, jnp.exp(scores), 0.0)
    denom_local = lax.optimization_barrier(jnp.sum(weights_local, axis=-1))
    pick = positions[:, None, None, None, None]
    query_int = jnp.take_along_axis(query, pick, axis=1)[:, 0]
    ext_scores = jnp.einsum('cngd,end->cnge', query_int.astype(jnp.float32), key_all.astype(jnp.float32)) * scale
    others = jnp.arange(key_all.shape[0])[None, :] != own_index[:, None]
    weights_ext = jnp.where(others[:, None, None, :], jnp.exp(ext_scores), 0.0)
    denom_ext = lax.optimization_barrier(jnp.sum(weights_ext, axis=-1))
    onehot = (slots[None, :] == positions[:, None]).astype(jnp.float32)
    denom_at = jnp.take_along_axis(denom_local, positions[:, None, None, None], axis=3)[..., 0] + denom_ext
    denom = denom_local + onehot[:, None, None, :] * denom_ext[..., None]
    probs_local = (weights_local / denom[..., None]).astype(jnp.bfloat16)
    probs_ext = (weights_ext / denom_at[..., None]).astype(jnp.bfloat16)
    out_local = jnp.einsum('cngst,ctnd->csngd', probs_local.astype(jnp.float32), vals.astype(jnp.float32))
    out_ext = jnp.einsum('cnge,end->cngd', probs_ext.astype(jnp.float32), value_all.astype(jnp.float32))
    mixed = out_local + onehot[:, :, None, None, None] * out_ext[:, None]
    return mixed.astype(jnp.bfloat16)

def reference(hidden_in, norm_gain, w_query, w_key, w_value, q_gain, k_gain, w_out, lengths, positions):
    values32 = hidden_in.astype(jnp.float32)
    inverse = lax.rsqrt(lax.optimization_barrier(jnp.mean(values32 * values32, axis=-1, keepdims=True)) + EPSILON)
    normed = (values32 * inverse * norm_gain).astype(jnp.bfloat16)
    query = jnp.dot(normed, w_query, preferred_element_type=jnp.float32)
    keys = jnp.dot(normed, w_key, preferred_element_type=jnp.float32)
    vals = jnp.dot(normed, w_value, preferred_element_type=jnp.float32)
    group_size = HEADS // KV_HEADS
    cosine, sine = rope_tables(SEQ, HD)
    query = head_norm(query.reshape(NCAND, SEQ, KV_HEADS, group_size, HD), q_gain)
    query = rotate(query, cosine[None, :, None, None, :], sine[None, :, None, None, :]).astype(jnp.bfloat16)
    keys = head_norm(keys.reshape(NCAND, SEQ, KV_HEADS, HD), k_gain)
    keys = rotate(keys, cosine[None, :, None, :], sine[None, :, None, :]).astype(jnp.bfloat16)
    vals = vals.reshape(NCAND, SEQ, KV_HEADS, HD).astype(jnp.bfloat16)
    pick = positions[:, None, None, None]
    key_int = jnp.take_along_axis(keys, pick, axis=1)[:, 0]
    value_int = jnp.take_along_axis(vals, pick, axis=1)[:, 0]
    own_index = jnp.arange(NCAND)
    mixed = attend(query, keys, vals, lengths, positions, key_int, value_int, own_index)
    mixed = mixed.reshape(ROWS, HEADS * HD)
    group_width = HEADS * HD // N_TP
    result = jnp.zeros((ROWS, D), jnp.float32)
    for index in range(N_TP):
        term = jnp.dot(mixed[:, index * group_width:(index + 1) * group_width], w_out[index * group_width:(index + 1) * group_width], preferred_element_type=jnp.float32)
        rounded = lax.optimization_barrier(term.astype(jnp.bfloat16))
        result = result + rounded.astype(jnp.float32)
    return result.astype(jnp.bfloat16)
```

```python
import functools

import jax
import jax.numpy as jnp
import numpy as np
from jax import lax
from jax.experimental import pallas as pl
from jax.experimental.pallas import tpu as pltpu
from jax.sharding import PartitionSpec as P

HD = 128
SEQ = 96
EPSILON = 1e-06
THETA = 1000000.0
F32, BF16 = jnp.float32, jnp.bfloat16
MESH = pl.DeviceIdType.MESH


def rope_tables():
    half = HD // 2
    frequency = np.float32(THETA) ** (-(np.arange(half, dtype=np.float32) * np.float32(2.0 / HD)))
    angles = np.arange(SEQ, dtype=np.float32)[:, None] * frequency.astype(np.float32)[None, :]
    cosine, sine = np.cos(angles), np.sin(angles)
    return (
        np.concatenate([cosine, cosine], axis=-1).astype(np.float32),
        np.concatenate([-sine, sine], axis=-1).astype(np.float32),
    )


def ring_plan(n, halves):
    far = n // 2
    if n == 1:
        return {1: [], -1: []}
    if halves == 1:
        return {
            1: [(d, 0) for d in range(1, far + 1)],
            -1: [(d, 0) for d in range(1, n - far)],
        }
    return {
        1: [(d, k) for d in range(1, far + 1) for k in (0, 1) if d < far or k == 0],
        -1: [(d, k) for d in range(1, far + 1) for k in (1, 0) if d < far or k == 1],
    }


class Sems:
    def __init__(self, send, recv):
        self.send, self.recv, self.used = send, recv, 0

    def take(self):
        self.used += 1
        return self.used - 1


class Ring:
    def __init__(self, n, me, slot, peer, sems, halves=2):
        self.n, self.me, self.slot, self.peer, self.sems = n, me, slot, peer, sems
        self.plan = ring_plan(n, halves)
        self.ids = {(s, *m): sems.take() for s in (1, -1) for m in self.plan[s]}
        self.rounds = max(len(self.plan[1]), len(self.plan[-1]))
        self.sent = []

    def at(self, offset):
        return lax.rem(self.me + offset + self.n, self.n)

    def copy(self, place, way, dist, half):
        ref, k = self.slot(place, half), self.ids[way, dist, half]
        return pltpu.make_async_remote_copy(
            src_ref=ref,
            dst_ref=ref,
            send_sem=self.sems.send.at[k],
            recv_sem=self.sems.recv.at[k],
            device_id=self.peer(self.at(way)),
            device_id_type=MESH,
        )

    def send(self, way, dist, half):
        copy = self.copy(self.at(-way * (dist - 1)), way, dist, half)
        copy.start()
        self.sent.append(copy)

    def start(self, half=None):
        for k in range(2):
            for way in (1, -1):
                mine = [m for m in self.plan[way] if m[0] == 1]
                if k < len(mine) and half in (None, mine[k][1]):
                    self.send(way, *mine[k])

    def event(self, r):
        got = []
        for way in (1, -1):
            if r < len(self.plan[way]):
                dist, half = self.plan[way][r]
                self.copy(self.at(-way * dist), way, dist, half).wait_recv()
                if (dist + 1, half) in self.plan[way]:
                    self.send(way, dist + 1, half)
                got.append((self.at(-way * dist), half))
        return got

    def finish(self):
        for copy in self.sent:
            copy.wait_send()


class Group:
    def __init__(self, *rings):
        self.rings = rings
        self.rounds = max(r.rounds for r in rings)

    def start(self):
        for ring in self.rings:
            ring.start()

    def event(self, *which):
        for r in which:
            for ring in self.rings:
                ring.event(r)

    def all(self):
        self.event(*range(self.rounds))

    def finish(self):
        for ring in self.rings:
            ring.finish()


class ChipGather:
    def __init__(self, n, x, core, cand, buf, rows, sems):
        def slot(i, half):
            return buf.at[i * 2 + core, pl.ds(half * rows, rows)]

        self.ring = Ring(n, x, slot, lambda i: (cand, i * 2 + core), sems)
        self.sems, self.buf, self.rows = sems, buf, rows
        self.n, self.x, self.core = n, x, core
        self.other = (cand, x * 2 + 1 - core)
        self.sent, self.due = [], []

    def pass_on(self, place, half):
        k = self.sems.take()
        mine = self.buf.at[place * 2 + self.core, pl.ds(half * self.rows, self.rows)]
        theirs = self.buf.at[place * 2 + 1 - self.core, pl.ds(half * self.rows, self.rows)]

        def copy(ref):
            return pltpu.make_async_remote_copy(
                src_ref=ref,
                dst_ref=ref,
                send_sem=self.sems.send.at[k],
                recv_sem=self.sems.recv.at[k],
                device_id=self.other,
                device_id_type=MESH,
            )

        out = copy(mine)
        out.start()
        self.sent.append(out)
        self.due.append(copy(theirs))

    def start(self, half=None):
        self.ring.start(half)
        for k in (0, 1):
            if half in (None, k):
                self.pass_on(self.x, k)

    def event(self, *which):
        for r in which:
            for place, half in self.ring.event(r):
                self.pass_on(place, half)

    def arrive(self):
        for copy in self.due:
            copy.wait_recv()

    def finish(self):
        self.ring.finish()
        for copy in self.sent:
            copy.wait_send()


def dot(a, b):
    return jnp.dot(a, b, preferred_element_type=F32)


def dot_t(a, b):
    return lax.dot_general(a, b, (((1,), (1,)), ((), ())), preferred_element_type=F32)


def iota(shape, axis):
    return lax.broadcasted_iota(jnp.int32, shape, axis)


def kernel(
    sizes,
    hidden,
    gain,
    w_query,
    w_key,
    w_value,
    q_gain,
    k_gain,
    w_out,
    lengths,
    positions,
    cosine,
    sine,
    out,
    hid,
    nrm,
    bk,
    bv,
    bqa,
    bqb,
    boa,
    bob,
    tokens,
    raw,
    turned,
    kbuf,
    vbuf,
    kacc,
    qacc,
    qbuf,
    mix,
    total,
    send,
    recv,
    local,
):
    Y, Z, X, TP, cands, group = sizes
    cand, t = lax.axis_index("cand"), lax.axis_index("tp")
    y, z = cand // Z, lax.rem(cand, Z)
    x, core = t // 2, lax.rem(t, 2)
    rows = cands * SEQ
    depth = w_key.shape[0]
    width = hidden.shape[1]
    half = depth // 2
    qh = group * HD // 2
    sems = Sems(send, recv)

    fetches = [
        pltpu.make_async_copy(src, dst, local.at[i])
        for i, (src, dst) in enumerate(
            [
                (w_key, bk.at[y, z]),
                (w_value, bv.at[y, z]),
                (hidden, hid.at[t]),
                (w_query.at[:, pl.ds(0, qh)], bqa.at[y, z]),
                (w_query.at[:, pl.ds(qh, qh)], bqb.at[y, z]),
                (w_out, raw),
            ]
        )
    ]
    for fetch in fetches:
        fetch.start()

    def along_y(i):
        return (i * Z + z, t)

    def along_z(i):
        return (y * Z + i, t)

    def along_x(i):
        return (cand, i * 2 + core)

    barrier = pltpu.get_barrier_semaphore()
    near = []
    for n, me, peer in ((Y, y, along_y), (Z, z, along_z), (X, x, along_x)):
        if n > 1:
            near += [peer(lax.rem(me + 1, n)), peer(lax.rem(me + n - 1, n))]
    swap = (t * Z + z, y)
    near += [(cand, x * 2 + 1 - core), swap]
    for peer in near:
        pl.semaphore_signal(barrier, inc=1, device_id=peer, device_id_type=MESH)
    pl.semaphore_wait(barrier, len(near))

    def gather(a, b):
        def part(k):
            return pl.ds(k * half, half)

        first = Group(
            Ring(Y, y, lambda i, k: a.at[i, z, part(k)], along_y, sems),
            Ring(Z, z, lambda i, k: b.at[y, i, part(k)], along_z, sems),
        )
        second = Group(
            Ring(Z, z, lambda i, k: a.at[:, i, part(k)], along_z, sems),
            Ring(Y, y, lambda i, k: b.at[i, :, part(k)], along_y, sems),
        )
        return first, second

    K1, K2 = gather(bk, bv)
    Q1, Q2 = gather(bqa, bqb)
    O1, O2 = gather(boa, bob)
    I1 = Group(Ring(Z, z, lambda i, k: tokens.at[y, i], along_z, sems, 1))
    I2 = Group(Ring(Y, y, lambda i, k: tokens.at[i], along_y, sems, 1))
    H = ChipGather(X, x, core, cand, hid, rows // 2, sems)
    M = ChipGather(X, x, core, cand, mix, rows // 2, sems)

    fetches[0].wait()
    fetches[1].wait()
    K1.start()
    fetches[2].wait()
    H.start()
    fetches[3].wait()
    fetches[4].wait()
    Q1.start()

    fetches[5].wait()
    eye = (iota((depth, depth), 0) == iota((depth, depth), 1)).astype(F32).astype(BF16)
    flat = dot_t(eye, raw[...]).astype(BF16)
    turned[0] = flat[:, :qh]
    turned[1] = flat[:, qh:]
    swaps = [sems.take(), sems.take()]

    def swap_copy(i, place):
        return pltpu.make_async_remote_copy(
            src_ref=turned.at[i],
            dst_ref=(boa, bob)[i].at[place, z],
            send_sem=send.at[swaps[i]],
            recv_sem=recv.at[swaps[i]],
            device_id=swap,
            device_id_type=MESH,
        )

    @pl.when(t != y)
    def _():
        for i in range(2):
            swap_copy(i, t).start()

    @pl.when(t == y)
    def _():
        for i in range(2):
            (boa, bob)[i][y, z] = turned[i]

    K1.all()
    K2.start()
    H.event(*range(0, min(1, H.ring.rounds)))
    Q1.all()
    K2.event(0, 1)
    H.event(*range(1, min(2, H.ring.rounds)))
    K2.event(2, 3, 4)
    Q2.start()
    H.event(*range(2, H.ring.rounds))
    K2.event(5, 6)

    @pl.when(t != y)
    def _():
        for i in range(2):
            swap_copy(i, y).wait_recv()

    O1.start()
    H.arrive()

    def squares(i, acc):
        v = hid[i].astype(F32)
        return acc + jnp.sum(v * v, axis=-1, keepdims=True)

    square = lax.fori_loop(0, TP, squares, jnp.zeros((rows, 1), F32))
    inverse = lax.rsqrt(square * (1.0 / (TP * width)) + EPSILON)

    def scale(i, carry):
        lanes = pl.ds(pl.multiple_of(i * width, 128), width)
        nrm[:, lanes] = (hid[i].astype(F32) * inverse * gain[:, lanes]).astype(BF16)
        return carry

    Q2.event(0)
    lax.fori_loop(0, TP, scale, 0)
    O1.event(0)
    Q2.event(1)

    def norm_rope(v, weight):
        v = v * lax.rsqrt(jnp.mean(v * v, axis=-1, keepdims=True) + EPSILON) * weight
        return (v * cosine[...] + pltpu.roll(v, HD // 2, 1) * sine[...]).astype(BF16)

    kacc[:, :HD] = dot(nrm[...], bk[...].reshape(TP * width, HD))
    kacc[:, HD:] = dot(nrm[...], bv[...].reshape(TP * width, HD))
    O1.event(1)
    Q2.event(2)
    pad = jnp.zeros((HD - SEQ, HD), BF16)
    picked = jnp.zeros((16, HD), F32)
    for j in range(cands):
        span = pl.ds(j * SEQ, SEQ)
        kj = norm_rope(kacc[span, :HD], k_gain[...])
        vj = kacc[span, HD:].astype(BF16)
        kbuf[j] = jnp.concatenate([kj, pad], axis=0)
        vbuf[j] = jnp.concatenate([vj, pad], axis=0)
        here = iota((16, HD), 1) == positions[j]
        for at, block in ((j, kbuf), (cands + j, vbuf)):
            sel = jnp.where(here & (iota((16, HD), 0) == at), 1.0, 0.0).astype(BF16)
            picked += dot(sel, block[j])
    tokens[y, z] = picked.astype(BF16)
    I1.start()
    O1.event(2)
    I1.event(0)
    Q2.event(3)
    I1.event(1)
    O1.event(3)
    I1.event(2)
    Q2.event(4)
    I1.event(3)
    I2.start()
    O1.event(4, 5)
    I2.event(0)
    Q2.event(5)
    I2.event(1)
    O1.event(6)
    O2.start()
    I2.event(2)
    Q2.event(6)

    qacc[:, :qh] = dot(nrm[...], bqa[...].reshape(TP * width, qh))
    I2.event(3)
    O2.event(0)
    qacc[:, qh:] = dot(nrm[...], bqb[...].reshape(TP * width, qh))
    asked = jnp.zeros((16, HD), F32)
    for j in range(cands):
        for h in range(group):
            qbuf[j, pl.ds(h * SEQ, SEQ)] = norm_rope(
                qacc[pl.ds(j * SEQ, SEQ), pl.ds(h * HD, HD)], q_gain[...]
            )
        shape = (16, group * SEQ)
        h = iota(shape, 0) - group * j
        here = (h >= 0) & (h < group) & (iota(shape, 1) == h * SEQ + positions[j])
        asked += dot(jnp.where(here, 1.0, 0.0).astype(BF16), qbuf[j])
    O2.event(1)

    factor = float(HD) ** (-0.5)
    flat = tokens[...].reshape(Y * Z * 16, HD)
    shape = (16, Y * Z * 16)
    column, row = iota(shape, 1), iota(shape, 0)
    inner = column & 15
    theirs = lax.shift_right_logical(column, 4) * cands + inner
    own = cand * cands + lax.div(row, jnp.int32(group))
    far = jnp.where(
        (inner < cands) & (theirs != own), jnp.exp(dot_t(asked.astype(BF16), flat) * factor), 0.0
    )
    far_den = jnp.sum(far, axis=-1, keepdims=True)
    far_sum = dot(pltpu.roll(far, cands, 1).astype(BF16), flat)

    slot_s, slot_t = iota((SEQ, HD), 0), iota((SEQ, HD), 1)
    for j in range(cands):
        allowed = (slot_t <= slot_s) & (slot_t < lengths[j])
        allowed = jnp.concatenate([allowed.astype(F32)] * group, axis=0) > 0.0
        scores = dot_t(qbuf[j], kbuf[j]) * factor
        e = jnp.where(allowed, jnp.exp(scores), 0.0)
        den = jnp.sum(e, axis=-1, keepdims=True)
        num = dot(e.astype(BF16), vbuf[j])
        for h in range(group):
            span = slice(h * SEQ, (h + 1) * SEQ)
            r = group * j + h
            here = slot_s == positions[j]
            d = den[span] + jnp.where(here, far_den[r : r + 1], 0.0)
            v = num[span] + jnp.where(here, far_sum[r : r + 1], 0.0)
            mix[t, pl.ds(j * SEQ, SEQ), pl.ds(h * HD, HD)] = (v / d).astype(BF16)
        if j == cands // 2 - 1:
            M.start(0)
            O2.event(2)
    M.start(1)
    O2.event(3)
    M.event(*range(0, min(1, M.ring.rounds)))
    O2.event(4)
    M.event(*range(1, min(2, M.ring.rounds)))
    O2.event(5)
    M.event(*range(2, M.ring.rounds))
    O2.event(6)
    M.arrive()

    total[...] = jnp.zeros_like(total)

    def project(i, carry):
        left = dot_t(mix[i, :, :qh], boa[i].reshape(width, qh))
        total[...] += left + dot_t(mix[i, :, qh:], bob[i].reshape(width, qh))
        return carry

    lax.fori_loop(0, TP, project, 0)
    out[...] = total[...].astype(BF16)

    for chain in (K1, K2, Q1, Q2, O1, O2, I1, I2, H, M):
        chain.finish()

    @pl.when(t != y)
    def _():
        for i in range(2):
            swap_copy(i, t).wait_send()


N_SEMS = 256


def shards(
    hidden_in, norm_gain, w_query, w_key, w_value, q_gain, k_gain, w_out, lengths, positions
):
    TP = lax.axis_size("tp")
    Y, Z, X = TP, lax.axis_size("cand") // TP, TP // 2
    rows, width = hidden_in.shape
    depth = w_key.shape[0]
    cands, group = rows // SEQ, w_query.shape[1] // w_key.shape[1]
    qh = group * HD // 2
    cosine, sine = rope_tables()
    any_, vmem, smem = (
        pl.BlockSpec(memory_space=m) for m in (pl.ANY, pltpu.VMEM, pltpu.SMEM)
    )
    return pl.pallas_call(
        functools.partial(kernel, (Y, Z, X, TP, cands, group)),
        out_shape=jax.ShapeDtypeStruct((rows, width), BF16),
        in_specs=[any_, vmem, any_, any_, any_, vmem, vmem, any_, smem, smem, vmem, vmem],
        out_specs=vmem,
        scratch_shapes=[
            pltpu.VMEM((TP, rows, width), BF16),
            pltpu.VMEM((rows, TP * width), BF16),
            pltpu.VMEM((Y, Z, depth, HD), BF16),
            pltpu.VMEM((Y, Z, depth, HD), BF16),
            pltpu.VMEM((Y, Z, depth, qh), BF16),
            pltpu.VMEM((Y, Z, depth, qh), BF16),
            pltpu.VMEM((Y, Z, depth, qh), BF16),
            pltpu.VMEM((Y, Z, depth, qh), BF16),
            pltpu.VMEM((Y, Z, 16, HD), BF16),
            pltpu.VMEM(w_out.shape, BF16),
            pltpu.VMEM((2, depth, qh), BF16),
            pltpu.VMEM((cands, HD, HD), BF16),
            pltpu.VMEM((cands, HD, HD), BF16),
            pltpu.VMEM((rows, 2 * HD), F32),
            pltpu.VMEM((rows, group * HD), F32),
            pltpu.VMEM((cands, group * SEQ, HD), BF16),
            pltpu.VMEM((TP, rows, group * HD), BF16),
            pltpu.VMEM((rows, width), F32),
            pltpu.SemaphoreType.DMA((N_SEMS,)),
            pltpu.SemaphoreType.DMA((N_SEMS,)),
            pltpu.SemaphoreType.DMA((6,)),
        ],
        compiler_params=pltpu.CompilerParams(
            collective_id=0, has_side_effects=True, vmem_limit_bytes=56 * 1024 * 1024
        ),
        cost_estimate=pl.CostEstimate(flops=4 * 10**9, bytes_accessed=2 * 10**6, transcendentals=10**6),
    )(
        hidden_in,
        norm_gain[None],
        w_query,
        w_key,
        w_value,
        q_gain[None],
        k_gain[None],
        w_out,
        lengths,
        positions,
        jnp.asarray(cosine),
        jnp.asarray(sine),
    )


def solution(mesh):
    in_specs = (
        P("cand", "tp"),
        P(),
        P("cand", "tp"),
        P("cand", "tp"),
        P("cand", "tp"),
        P(),
        P(),
        P("tp", "cand"),
        P("cand"),
        P("cand"),
    )
    out_specs = P("cand", "tp")
    return jax.shard_map(shards, mesh=mesh, in_specs=in_specs, out_specs=out_specs, check_vma=False)
```

```python
import functools

import jax
import jax.numpy as jnp
import numpy as np
from jax import lax
from jax.experimental import pallas as pl
from jax.experimental.pallas import tpu as pltpu
from jax.sharding import PartitionSpec as P

HD = 128
SEQ = 96
EPSILON = 1e-06
THETA = 1000000.0
F32, BF16 = jnp.float32, jnp.bfloat16
MESH = pl.DeviceIdType.MESH


def rope_tables():
    half = HD // 2
    frequency = np.float32(THETA) ** (-(np.arange(half, dtype=np.float32) * np.float32(2.0 / HD)))
    angles = np.arange(SEQ, dtype=np.float32)[:, None] * frequency.astype(np.float32)[None, :]
    cosine, sine = np.cos(angles), np.sin(angles)
    return (
        np.concatenate([cosine, cosine], axis=-1).astype(np.float32),
        np.concatenate([-sine, sine], axis=-1).astype(np.float32),
    )


def ring_plan(n, halves):
    far = n // 2
    if n == 1:
        return {1: [], -1: []}
    if halves == 1:
        return {
            1: [(d, 0) for d in range(1, far + 1)],
            -1: [(d, 0) for d in range(1, n - far)],
        }
    return {
        1: [(d, k) for d in range(1, far + 1) for k in (0, 1) if d < far or k == 0],
        -1: [(d, k) for d in range(1, far + 1) for k in (1, 0) if d < far or k == 1],
    }


class Sems:
    def __init__(self, send, recv):
        self.send, self.recv, self.used = send, recv, 0

    def take(self):
        self.used += 1
        return self.used - 1


class Ring:
    def __init__(self, n, me, slot, peer, sems, halves=2):
        self.n, self.me, self.slot, self.peer, self.sems = n, me, slot, peer, sems
        self.plan = ring_plan(n, halves)
        self.ids = {(s, *m): sems.take() for s in (1, -1) for m in self.plan[s]}
        self.rounds = max(len(self.plan[1]), len(self.plan[-1]))
        self.sent = []

    def at(self, offset):
        return lax.rem(self.me + offset + self.n, self.n)

    def copy(self, place, way, dist, half):
        ref, k = self.slot(place, half), self.ids[way, dist, half]
        return pltpu.make_async_remote_copy(
            src_ref=ref,
            dst_ref=ref,
            send_sem=self.sems.send.at[k],
            recv_sem=self.sems.recv.at[k],
            device_id=self.peer(self.at(way)),
            device_id_type=MESH,
        )

    def send(self, way, dist, half):
        copy = self.copy(self.at(-way * (dist - 1)), way, dist, half)
        copy.start()
        self.sent.append(copy)

    def start(self, half=None):
        for k in range(2):
            for way in (1, -1):
                mine = [m for m in self.plan[way] if m[0] == 1]
                if k < len(mine) and half in (None, mine[k][1]):
                    self.send(way, *mine[k])

    def event(self, r):
        got = []
        for way in (1, -1):
            if r < len(self.plan[way]):
                dist, half = self.plan[way][r]
                self.copy(self.at(-way * dist), way, dist, half).wait_recv()
                if (dist + 1, half) in self.plan[way]:
                    self.send(way, dist + 1, half)
                got.append((self.at(-way * dist), half))
        return got

    def finish(self):
        for copy in self.sent:
            copy.wait_send()


class Group:
    def __init__(self, *rings):
        self.rings = rings
        self.rounds = max(getattr(r, "rounds", 0) for r in rings)

    def start(self):
        for ring in self.rings:
            ring.start()

    def event(self, *which):
        for r in which:
            for ring in self.rings:
                ring.event(r)

    def all(self):
        self.event(*range(self.rounds))

    def arrive(self):
        for ring in self.rings:
            ring.arrive()

    def finish(self):
        for ring in self.rings:
            ring.finish()


class Direct:
    def __init__(self, n, me, slot, peer, sems):
        self.n, self.me, self.slot, self.peer, self.sems = n, me, slot, peer, sems
        self.order = sorted(range(1, n), key=lambda d: (min(d, n - d), d))
        self.ids = {d: sems.take() for d in self.order}
        self.sent = []

    def copy(self, dist, place):
        ref = self.slot(place)
        return pltpu.make_async_remote_copy(
            src_ref=ref,
            dst_ref=ref,
            send_sem=self.sems.send.at[self.ids[dist]],
            recv_sem=self.sems.recv.at[self.ids[dist]],
            device_id=self.peer(lax.rem(self.me + dist, self.n)),
            device_id_type=MESH,
        )

    def start(self):
        for dist in reversed(self.order):
            copy = self.copy(dist, self.me)
            copy.start()
            self.sent.append(copy)

    def arrive(self):
        for dist in self.order:
            self.copy(dist, lax.rem(self.me - dist + self.n, self.n)).wait_recv()

    def finish(self):
        for copy in self.sent:
            copy.wait_send()


class ChipGather:
    def __init__(self, n, x, core, cand, buf, rows, sems):
        def slot(i, half):
            return buf.at[i * 2 + core, pl.ds(half * rows, rows)]

        self.ring = Ring(n, x, slot, lambda i: (cand, i * 2 + core), sems)
        self.sems, self.buf, self.rows = sems, buf, rows
        self.n, self.x, self.core = n, x, core
        self.other = (cand, x * 2 + 1 - core)
        self.sent, self.due = [], []

    def pass_on(self, place, half):
        k = self.sems.take()
        mine = self.buf.at[place * 2 + self.core, pl.ds(half * self.rows, self.rows)]
        theirs = self.buf.at[place * 2 + 1 - self.core, pl.ds(half * self.rows, self.rows)]

        def copy(ref):
            return pltpu.make_async_remote_copy(
                src_ref=ref,
                dst_ref=ref,
                send_sem=self.sems.send.at[k],
                recv_sem=self.sems.recv.at[k],
                device_id=self.other,
                device_id_type=MESH,
            )

        out = copy(mine)
        out.start()
        self.sent.append(out)
        self.due.append(copy(theirs))

    def start(self, half=None):
        self.ring.start(half)
        for k in (0, 1):
            if half in (None, k):
                self.pass_on(self.x, k)

    def event(self, *which):
        for r in which:
            for place, half in self.ring.event(r):
                self.pass_on(place, half)

    def arrive(self):
        for copy in self.due:
            copy.wait_recv()

    def finish(self):
        self.ring.finish()
        for copy in self.sent:
            copy.wait_send()


def dot(a, b):
    return jnp.dot(a, b, preferred_element_type=F32)


def dot_t(a, b):
    return lax.dot_general(a, b, (((1,), (1,)), ((), ())), preferred_element_type=F32)


def iota(shape, axis):
    return lax.broadcasted_iota(jnp.int32, shape, axis)


def kernel(
    sizes,
    hidden,
    gain,
    w_query,
    w_key,
    w_value,
    q_gain,
    k_gain,
    w_out,
    lengths,
    positions,
    cosine,
    sine,
    out,
    hid,
    nrm,
    bk,
    bv,
    bqa,
    bqb,
    boa,
    bob,
    tokens,
    raw,
    kbuf,
    vbuf,
    kacc,
    qacc,
    qbuf,
    mix,
    total,
    send,
    recv,
    local,
):
    Y, Z, X, TP, cands, group = sizes
    cand, t = lax.axis_index("cand"), lax.axis_index("tp")
    y, z = cand // Z, lax.rem(cand, Z)
    x, core = t // 2, lax.rem(t, 2)
    rows = cands * SEQ
    depth = w_key.shape[0]
    width = hidden.shape[1]
    half = depth // 2
    qh = group * HD // 2
    sems = Sems(send, recv)

    fetches = [
        pltpu.make_async_copy(src, dst, local.at[i])
        for i, (src, dst) in enumerate(
            [
                (w_key, bk.at[y, z]),
                (w_value, bv.at[y, z]),
                (hidden, hid.at[t]),
                (w_query.at[:, pl.ds(0, qh)], bqa.at[y, z]),
                (w_query.at[:, pl.ds(qh, qh)], bqb.at[y, z]),
                (w_out, raw),
            ]
        )
    ]
    for fetch in fetches:
        fetch.start()

    def along_y(i):
        return (i * Z + z, t)

    def along_z(i):
        return (y * Z + i, t)

    def along_x(i):
        return (cand, i * 2 + core)

    barrier = pltpu.get_barrier_semaphore()
    near = []
    for n, me, peer in ((Y, y, along_y), (Z, z, along_z)):
        near += [peer(lax.rem(me + i, n)) for i in range(1, n)]
    if X > 1:
        near += [along_x(lax.rem(x + 1, X)), along_x(lax.rem(x + X - 1, X))]
    swap = (t * Z + z, y)
    near += [(cand, x * 2 + 1 - core), swap]
    for peer in near:
        pl.semaphore_signal(barrier, inc=1, device_id=peer, device_id_type=MESH)
    pl.semaphore_wait(barrier, len(near))

    def gather(a, b, direct):
        def part(k):
            return pl.ds(k * half, half)

        if direct:
            first = Group(
                Direct(Y, y, lambda i: a.at[i, z], along_y, sems),
                Direct(Z, z, lambda i: b.at[y, i], along_z, sems),
            )
        else:
            first = Group(
                Ring(Y, y, lambda i, k: a.at[i, z, part(k)], along_y, sems),
                Ring(Z, z, lambda i, k: b.at[y, i, part(k)], along_z, sems),
            )
        second = Group(
            Ring(Z, z, lambda i, k: a.at[:, i, part(k)], along_z, sems),
            Ring(Y, y, lambda i, k: b.at[i, :, part(k)], along_y, sems),
        )
        return first, second

    K1, K2 = gather(bk, bv, True)
    Q1, Q2 = gather(bqa, bqb, True)
    O1, O2 = gather(boa, bob, False)
    I1 = Direct(Z, z, lambda i: tokens.at[y, i], along_z, sems)
    I2 = Direct(Y, y, lambda i: tokens.at[i], along_y, sems)
    H = ChipGather(X, x, core, cand, hid, rows // 2, sems)
    M = ChipGather(X, x, core, cand, mix, rows // 2, sems)

    fetches[0].wait()
    fetches[1].wait()
    K1.start()
    fetches[2].wait()
    H.start()
    fetches[3].wait()
    fetches[4].wait()
    Q1.start()

    fetches[5].wait()
    swaps = [sems.take(), sems.take()]

    def swap_copy(i, place):
        return pltpu.make_async_remote_copy(
            src_ref=raw.at[:, pl.ds(i * qh, qh)],
            dst_ref=(boa, bob)[i].at[place, z],
            send_sem=send.at[swaps[i]],
            recv_sem=recv.at[swaps[i]],
            device_id=swap,
            device_id_type=MESH,
        )

    @pl.when(t != y)
    def _():
        for i in range(2):
            swap_copy(i, t).start()

    @pl.when(t == y)
    def _():
        for i in range(2):
            (boa, bob)[i][y, z] = raw[:, pl.ds(i * qh, qh)]

    def steps(gather, r):
        if r < gather.ring.rounds:
            gather.event(r)

    K1.arrive()
    K2.start()
    steps(H, 0)
    Q1.arrive()
    K2.event(0, 1)

    @pl.when(t != y)
    def _():
        for i in range(2):
            swap_copy(i, y).wait_recv()

    steps(H, 1)
    K2.event(2)
    Q2.start()
    K2.event(3, 4)
    steps(H, 2)
    O1.start()
    K2.event(5)
    H.arrive()

    def squares(i, acc):
        v = hid[i].astype(F32)
        return acc + jnp.sum(v * v, axis=-1, keepdims=True)

    square = lax.fori_loop(0, TP, squares, jnp.zeros((rows, 1), F32))
    inverse = lax.rsqrt(square * (1.0 / (TP * width)) + EPSILON)

    def scale(i, carry):
        lanes = pl.ds(pl.multiple_of(i * width, 128), width)
        nrm[:, lanes] = (hid[i].astype(F32) * inverse * gain[:, lanes]).astype(BF16)
        return carry

    K2.event(6)
    lax.fori_loop(0, TP, scale, 0)
    Q2.event(0)
    O1.event(0)

    def norm_rope(v, weight):
        v = v * lax.rsqrt(jnp.mean(v * v, axis=-1, keepdims=True) + EPSILON) * weight
        return (v * cosine[...] + pltpu.roll(v, HD // 2, 1) * sine[...]).astype(BF16)

    kacc[:, :HD] = dot(nrm[...], bk[...].reshape(TP * width, HD))
    kacc[:, HD:] = dot(nrm[...], bv[...].reshape(TP * width, HD))
    Q2.event(1)
    O1.event(1, 2)
    pad = jnp.zeros((HD - SEQ, HD), BF16)
    picked = jnp.zeros((16, HD), F32)
    for j in range(cands):
        span = pl.ds(j * SEQ, SEQ)
        kj = norm_rope(kacc[span, :HD], k_gain[...])
        vj = kacc[span, HD:].astype(BF16)
        kbuf[j] = jnp.concatenate([kj, pad], axis=0)
        vbuf[j] = jnp.concatenate([vj, pad], axis=0)
        here = iota((16, HD), 1) == positions[j]
        for at, block in ((j, kbuf), (cands + j, vbuf)):
            sel = jnp.where(here & (iota((16, HD), 0) == at), 1.0, 0.0).astype(BF16)
            picked += dot(sel, block[j])
    tokens[y, z] = picked.astype(BF16)
    I1.start()
    Q2.event(2)
    O1.event(3, 4, 5, 6)
    Q2.event(3)
    I1.arrive()
    I2.start()
    Q2.event(4)
    O2.start()
    Q2.event(5)
    Q2.event(6)

    qacc[:, :qh] = dot(nrm[...], bqa[...].reshape(TP * width, qh))
    O2.event(0)
    qacc[:, qh:] = dot(nrm[...], bqb[...].reshape(TP * width, qh))
    asked = jnp.zeros((16, HD), F32)
    for j in range(cands):
        for h in range(group):
            qbuf[j, pl.ds(h * SEQ, SEQ)] = norm_rope(
                qacc[pl.ds(j * SEQ, SEQ), pl.ds(h * HD, HD)], q_gain[...]
            )
        shape = (16, group * SEQ)
        h = iota(shape, 0) - group * j
        here = (h >= 0) & (h < group) & (iota(shape, 1) == h * SEQ + positions[j])
        asked += dot(jnp.where(here, 1.0, 0.0).astype(BF16), qbuf[j])
    O2.event(1)
    I2.arrive()

    factor = float(HD) ** (-0.5)
    flat = tokens[...].reshape(Y * Z * 16, HD)
    shape = (16, Y * Z * 16)
    column, row = iota(shape, 1), iota(shape, 0)
    inner = column & 15
    theirs = lax.shift_right_logical(column, 4) * cands + inner
    own = cand * cands + lax.div(row, jnp.int32(group))
    far = jnp.where(
        (inner < cands) & (theirs != own), jnp.exp(dot_t(asked.astype(BF16), flat) * factor), 0.0
    )
    far_den = jnp.sum(far, axis=-1, keepdims=True)
    far_sum = dot(pltpu.roll(far, cands, 1).astype(BF16), flat)

    slot_s, slot_t = iota((SEQ, HD), 0), iota((SEQ, HD), 1)
    for j in range(cands):
        allowed = (slot_t <= slot_s) & (slot_t < lengths[j])
        allowed = jnp.concatenate([allowed.astype(F32)] * group, axis=0) > 0.0
        scores = dot_t(qbuf[j], kbuf[j]) * factor
        e = jnp.where(allowed, jnp.exp(scores), 0.0)
        den = jnp.sum(e, axis=-1, keepdims=True)
        num = dot(e.astype(BF16), vbuf[j])
        for h in range(group):
            span = slice(h * SEQ, (h + 1) * SEQ)
            r = group * j + h
            here = slot_s == positions[j]
            d = den[span] + jnp.where(here, far_den[r : r + 1], 0.0)
            v = num[span] + jnp.where(here, far_sum[r : r + 1], 0.0)
            mix[t, pl.ds(j * SEQ, SEQ), pl.ds(h * HD, HD)] = (v / d).astype(BF16)
        if j == cands // 2 - 1:
            M.start(0)
            O2.event(2)
    M.start(1)
    O2.event(3)
    steps(M, 0)
    O2.event(4)
    steps(M, 1)
    O2.event(5)
    steps(M, 2)
    O2.event(6)
    M.arrive()

    total[...] = jnp.zeros_like(total)

    def project(i, carry):
        left = dot_t(mix[i, :, :qh], boa[i].reshape(width, qh))
        total[...] += left + dot_t(mix[i, :, qh:], bob[i].reshape(width, qh))
        return carry

    lax.fori_loop(0, TP, project, 0)
    out[...] = total[...].astype(BF16)

    for chain in (K1, K2, Q1, Q2, O1, O2, I1, I2, H, M):
        chain.finish()

    @pl.when(t != y)
    def _():
        for i in range(2):
            swap_copy(i, t).wait_send()


N_SEMS = 256


def shards(
    hidden_in, norm_gain, w_query, w_key, w_value, q_gain, k_gain, w_out, lengths, positions
):
    TP = lax.axis_size("tp")
    Y, Z, X = TP, lax.axis_size("cand") // TP, TP // 2
    rows, width = hidden_in.shape
    depth = w_key.shape[0]
    cands, group = rows // SEQ, w_query.shape[1] // w_key.shape[1]
    qh = group * HD // 2
    cosine, sine = rope_tables()
    any_, vmem, smem = (
        pl.BlockSpec(memory_space=m) for m in (pl.ANY, pltpu.VMEM, pltpu.SMEM)
    )
    return pl.pallas_call(
        functools.partial(kernel, (Y, Z, X, TP, cands, group)),
        out_shape=jax.ShapeDtypeStruct((rows, width), BF16),
        in_specs=[any_, vmem, any_, any_, any_, vmem, vmem, any_, smem, smem, vmem, vmem],
        out_specs=vmem,
        scratch_shapes=[
            pltpu.VMEM((TP, rows, width), BF16),
            pltpu.VMEM((rows, TP * width), BF16),
            pltpu.VMEM((Y, Z, depth, HD), BF16),
            pltpu.VMEM((Y, Z, depth, HD), BF16),
            pltpu.VMEM((Y, Z, depth, qh), BF16),
            pltpu.VMEM((Y, Z, depth, qh), BF16),
            pltpu.VMEM((Y, Z, depth, qh), BF16),
            pltpu.VMEM((Y, Z, depth, qh), BF16),
            pltpu.VMEM((Y, Z, 16, HD), BF16),
            pltpu.VMEM((depth, 2 * qh), BF16),
            pltpu.VMEM((cands, HD, HD), BF16),
            pltpu.VMEM((cands, HD, HD), BF16),
            pltpu.VMEM((rows, 2 * HD), F32),
            pltpu.VMEM((rows, group * HD), F32),
            pltpu.VMEM((cands, group * SEQ, HD), BF16),
            pltpu.VMEM((TP, rows, group * HD), BF16),
            pltpu.VMEM((rows, width), F32),
            pltpu.SemaphoreType.DMA((N_SEMS,)),
            pltpu.SemaphoreType.DMA((N_SEMS,)),
            pltpu.SemaphoreType.DMA((6,)),
        ],
        compiler_params=pltpu.CompilerParams(
            collective_id=0, has_side_effects=True, vmem_limit_bytes=56 * 1024 * 1024
        ),
        cost_estimate=pl.CostEstimate(flops=4 * 10**9, bytes_accessed=2 * 10**6, transcendentals=10**6),
    )(
        hidden_in,
        norm_gain[None],
        w_query,
        w_key,
        w_value,
        q_gain[None],
        k_gain[None],
        w_out.T,
        lengths,
        positions,
        jnp.asarray(cosine),
        jnp.asarray(sine),
    )


def solution(mesh):
    in_specs = (
        P("cand", "tp"),
        P(),
        P("cand", "tp"),
        P("cand", "tp"),
        P("cand", "tp"),
        P(),
        P(),
        P("tp", "cand"),
        P("cand"),
        P("cand"),
    )
    out_specs = P("cand", "tp")
    return jax.shard_map(shards, mesh=mesh, in_specs=in_specs, out_specs=out_specs, check_vma=False)
```

```python
import functools

import jax
import jax.numpy as jnp
import numpy as np
from jax import lax
from jax.experimental import pallas as pl
from jax.experimental.pallas import tpu as pltpu
from jax.sharding import PartitionSpec as P

HD = 128
SEQ = 96
EPSILON = 1e-06
THETA = 1000000.0
F32, BF16 = jnp.float32, jnp.bfloat16
MESH = pl.DeviceIdType.MESH


def rope_tables():
    half = HD // 2
    frequency = np.float32(THETA) ** (-(np.arange(half, dtype=np.float32) * np.float32(2.0 / HD)))
    angles = np.arange(SEQ, dtype=np.float32)[:, None] * frequency.astype(np.float32)[None, :]
    cosine, sine = np.cos(angles), np.sin(angles)
    return (
        np.concatenate([cosine, cosine], axis=-1).astype(np.float32),
        np.concatenate([-sine, sine], axis=-1).astype(np.float32),
    )


def ring_plan(n, halves):
    far = n // 2
    if n == 1:
        return {1: [], -1: []}
    if halves == 1:
        return {
            1: [(d, 0) for d in range(1, far + 1)],
            -1: [(d, 0) for d in range(1, n - far)],
        }
    return {
        1: [(d, k) for d in range(1, far + 1) for k in (0, 1) if d < far or k == 0],
        -1: [(d, k) for d in range(1, far + 1) for k in (1, 0) if d < far or k == 1],
    }


class Sems:
    def __init__(self, send, recv):
        self.send, self.recv, self.used = send, recv, 0

    def take(self):
        self.used += 1
        return self.used - 1


class Ring:
    def __init__(self, n, me, slot, peer, sems, halves=2):
        self.n, self.me, self.slot, self.peer, self.sems = n, me, slot, peer, sems
        self.plan = ring_plan(n, halves)
        self.ids = {(s, *m): sems.take() for s in (1, -1) for m in self.plan[s]}
        self.rounds = max(len(self.plan[1]), len(self.plan[-1]))
        self.sent = []

    def at(self, offset):
        return lax.rem(self.me + offset + self.n, self.n)

    def copy(self, place, way, dist, half):
        ref, k = self.slot(place, half), self.ids[way, dist, half]
        return pltpu.make_async_remote_copy(
            src_ref=ref,
            dst_ref=ref,
            send_sem=self.sems.send.at[k],
            recv_sem=self.sems.recv.at[k],
            device_id=self.peer(self.at(way)),
            device_id_type=MESH,
        )

    def send(self, way, dist, half):
        copy = self.copy(self.at(-way * (dist - 1)), way, dist, half)
        copy.start()
        self.sent.append(copy)

    def start(self, half=None):
        for k in range(2):
            for way in (1, -1):
                mine = [m for m in self.plan[way] if m[0] == 1]
                if k < len(mine) and half in (None, mine[k][1]):
                    self.send(way, *mine[k])

    def event(self, r):
        got = []
        for way in (1, -1):
            if r < len(self.plan[way]):
                dist, half = self.plan[way][r]
                self.copy(self.at(-way * dist), way, dist, half).wait_recv()
                if (dist + 1, half) in self.plan[way]:
                    self.send(way, dist + 1, half)
                got.append((self.at(-way * dist), half))
        return got

    def finish(self):
        for copy in self.sent:
            copy.wait_send()


class Group:
    def __init__(self, *rings):
        self.rings = rings
        self.rounds = max(getattr(r, "rounds", 0) for r in rings)

    def start(self):
        for ring in self.rings:
            ring.start()

    def event(self, *which):
        for r in which:
            for ring in self.rings:
                ring.event(r)

    def all(self):
        self.event(*range(self.rounds))

    def arrive(self):
        for ring in self.rings:
            ring.arrive()

    def finish(self):
        for ring in self.rings:
            ring.finish()


class Direct:
    def __init__(self, n, me, slot, peer, sems):
        self.n, self.me, self.slot, self.peer, self.sems = n, me, slot, peer, sems
        self.order = sorted(range(1, n), key=lambda d: (min(d, n - d), d))
        self.ids = {d: sems.take() for d in self.order}
        self.sent = []

    def copy(self, dist, place):
        ref = self.slot(place)
        return pltpu.make_async_remote_copy(
            src_ref=ref,
            dst_ref=ref,
            send_sem=self.sems.send.at[self.ids[dist]],
            recv_sem=self.sems.recv.at[self.ids[dist]],
            device_id=self.peer(lax.rem(self.me + dist, self.n)),
            device_id_type=MESH,
        )

    def start(self):
        for dist in reversed(self.order):
            copy = self.copy(dist, self.me)
            copy.start()
            self.sent.append(copy)

    def arrive(self):
        for dist in self.order:
            self.copy(dist, lax.rem(self.me - dist + self.n, self.n)).wait_recv()

    def finish(self):
        for copy in self.sent:
            copy.wait_send()


class ChipGather:
    def __init__(self, n, x, core, cand, buf, rows, sems):
        def slot(i, half):
            return buf.at[i * 2 + core, pl.ds(half * rows, rows)]

        self.ring = Ring(n, x, slot, lambda i: (cand, i * 2 + core), sems)
        self.sems, self.buf, self.rows = sems, buf, rows
        self.n, self.x, self.core = n, x, core
        self.other = (cand, x * 2 + 1 - core)
        self.sent, self.due = [], []

    def pass_on(self, place, half):
        k = self.sems.take()
        mine = self.buf.at[place * 2 + self.core, pl.ds(half * self.rows, self.rows)]
        theirs = self.buf.at[place * 2 + 1 - self.core, pl.ds(half * self.rows, self.rows)]

        def copy(ref):
            return pltpu.make_async_remote_copy(
                src_ref=ref,
                dst_ref=ref,
                send_sem=self.sems.send.at[k],
                recv_sem=self.sems.recv.at[k],
                device_id=self.other,
                device_id_type=MESH,
            )

        out = copy(mine)
        out.start()
        self.sent.append(out)
        self.due.append(copy(theirs))

    def start(self, half=None):
        self.ring.start(half)
        for k in (0, 1):
            if half in (None, k):
                self.pass_on(self.x, k)

    def event(self, *which):
        for r in which:
            for place, half in self.ring.event(r):
                self.pass_on(place, half)

    def arrive(self):
        for copy in self.due:
            copy.wait_recv()

    def finish(self):
        self.ring.finish()
        for copy in self.sent:
            copy.wait_send()


def dot(a, b):
    return jnp.dot(a, b, preferred_element_type=F32)


def dot_t(a, b):
    return lax.dot_general(a, b, (((1,), (1,)), ((), ())), preferred_element_type=F32)


def iota(shape, axis):
    return lax.broadcasted_iota(jnp.int32, shape, axis)


def kernel(
    sizes,
    hidden,
    gain,
    w_query,
    w_key,
    w_value,
    q_gain,
    k_gain,
    w_out,
    lengths,
    positions,
    cosine,
    sine,
    out,
    hid,
    nrm,
    bk,
    bv,
    bqa,
    bqb,
    boa,
    bob,
    key_row,
    value_row,
    key_all,
    value_all,
    raw,
    kbuf,
    vbuf,
    kacc,
    qacc,
    qbuf,
    mix,
    total,
    near_den,
    near_sum,
    send,
    recv,
    local,
):
    Y, Z, X, TP, cands, group = sizes
    cand, t = lax.axis_index("cand"), lax.axis_index("tp")
    y, z = cand // Z, lax.rem(cand, Z)
    x, core = t // 2, lax.rem(t, 2)
    rows = cands * SEQ
    depth = w_key.shape[0]
    width = hidden.shape[1]
    half = depth // 2
    qh = group * HD // 2
    sems = Sems(send, recv)

    fetches = [
        pltpu.make_async_copy(src, dst, local.at[i])
        for i, (src, dst) in enumerate(
            [
                (w_key, bk.at[y, z]),
                (w_value, bv.at[y, z]),
                (hidden, hid.at[t]),
                (w_query.at[:, pl.ds(0, qh)], bqa.at[y, z]),
                (w_query.at[:, pl.ds(qh, qh)], bqb.at[y, z]),
                (w_out, raw),
            ]
        )
    ]
    for fetch in fetches:
        fetch.start()

    def along_y(i):
        return (i * Z + z, t)

    def along_z(i):
        return (y * Z + i, t)

    def along_tp(i):
        return (cand, i)

    barrier = pltpu.get_barrier_semaphore()
    near = []
    for n, me, peer in ((Y, y, along_y), (Z, z, along_z)):
        near += [peer(lax.rem(me + i, n)) for i in range(1, n)]
    near += [along_tp(lax.rem(t + i, TP)) for i in range(1, TP)]
    swap = (t * Z + z, y)
    near.append(swap)
    for peer in near:
        pl.semaphore_signal(barrier, inc=1, device_id=peer, device_id_type=MESH)
    pl.semaphore_wait(barrier, len(near))

    def gather(a, b, direct):
        def part(k):
            return pl.ds(k * half, half)

        if direct:
            first = Group(
                Direct(Y, y, lambda i: a.at[i, z], along_y, sems),
                Direct(Z, z, lambda i: b.at[y, i], along_z, sems),
            )
        else:
            first = Group(
                Ring(Y, y, lambda i, k: a.at[i, z, part(k)], along_y, sems),
                Ring(Z, z, lambda i, k: b.at[y, i, part(k)], along_z, sems),
            )
        second = Group(
            Ring(Z, z, lambda i, k: a.at[:, i, part(k)], along_z, sems),
            Ring(Y, y, lambda i, k: b.at[i, :, part(k)], along_y, sems),
        )
        return first, second

    K1, K2 = gather(bk, bv, True)
    Q1, Q2 = gather(bqa, bqb, True)
    O1, O2 = gather(boa, bob, False)
    I1 = Group(
        Direct(Z, z, lambda i: key_row.at[i], along_z, sems),
        Direct(Y, y, lambda i: value_row.at[i], along_y, sems),
    )
    I2 = Group(
        Direct(Y, y, lambda i: key_all.at[i], along_y, sems),
        Direct(Z, z, lambda i: value_all.at[i], along_z, sems),
    )
    H = ChipGather(X, x, core, cand, hid, rows // 2, sems)
    T = Direct(TP, t, lambda i: mix.at[i, pl.ds(rows, 16)], along_tp, sems)
    M = ChipGather(X, x, core, cand, mix, rows // 2, sems)

    fetches[0].wait()
    fetches[1].wait()
    K1.start()
    fetches[2].wait()
    H.start()
    fetches[3].wait()
    fetches[4].wait()
    Q1.start()

    fetches[5].wait()
    swaps = [sems.take(), sems.take()]

    def swap_copy(i, place):
        return pltpu.make_async_remote_copy(
            src_ref=raw.at[:, pl.ds(i * qh, qh)],
            dst_ref=(boa, bob)[i].at[place, z],
            send_sem=send.at[swaps[i]],
            recv_sem=recv.at[swaps[i]],
            device_id=swap,
            device_id_type=MESH,
        )

    @pl.when(t != y)
    def _():
        for i in range(2):
            swap_copy(i, t).start()

    @pl.when(t == y)
    def _():
        for i in range(2):
            (boa, bob)[i][y, z] = raw[:, pl.ds(i * qh, qh)]

    def steps(gather, r):
        if r < gather.ring.rounds:
            gather.event(r)

    K1.arrive()
    K2.start()
    steps(H, 0)
    Q1.arrive()
    K2.event(0, 1)

    @pl.when(t != y)
    def _():
        for i in range(2):
            swap_copy(i, y).wait_recv()

    steps(H, 1)
    K2.event(2)
    Q2.start()
    K2.event(3, 4)
    steps(H, 2)
    O1.start()
    K2.event(5)
    H.arrive()

    def squares(i, acc):
        v = hid[i].astype(F32)
        return acc + jnp.sum(v * v, axis=-1, keepdims=True)

    square = lax.fori_loop(0, TP, squares, jnp.zeros((rows, 1), F32))
    inverse = lax.rsqrt(square * (1.0 / (TP * width)) + EPSILON)

    def scale(i, carry):
        lanes = pl.ds(pl.multiple_of(i * width, 128), width)
        nrm[:, lanes] = (hid[i].astype(F32) * inverse * gain[:, lanes]).astype(BF16)
        return carry

    K2.event(6)
    lax.fori_loop(0, TP, scale, 0)
    Q2.event(0)
    O1.event(0)

    def norm_rope(v, weight):
        v = v * lax.rsqrt(jnp.mean(v * v, axis=-1, keepdims=True) + EPSILON) * weight
        return (v * cosine[...] + pltpu.roll(v, HD // 2, 1) * sine[...]).astype(BF16)

    kacc[:, :HD] = dot(nrm[...], bk[...].reshape(TP * width, HD))
    kacc[:, HD:] = dot(nrm[...], bv[...].reshape(TP * width, HD))
    Q2.event(1)
    O1.event(1, 2)
    pad = jnp.zeros((HD - SEQ, HD), BF16)
    picked = [jnp.zeros((16, HD), F32)] * 2
    for j in range(cands):
        span = pl.ds(j * SEQ, SEQ)
        kj = norm_rope(kacc[span, :HD], k_gain[...])
        vj = kacc[span, HD:].astype(BF16)
        kbuf[j] = jnp.concatenate([kj, pad], axis=0)
        vbuf[j] = jnp.concatenate([vj, pad], axis=0)
        here = iota((16, HD), 1) == positions[j]
        sel = jnp.where(here & (iota((16, HD), 0) == j), 1.0, 0.0).astype(BF16)
        picked = [p + dot(sel, block[j]) for p, block in zip(picked, (kbuf, vbuf))]
    key_row[z] = picked[0].astype(BF16)
    value_row[y] = picked[1].astype(BF16)
    I1.start()
    Q2.event(2)
    O1.event(3, 4, 5, 6)
    Q2.event(3, 4)
    O2.start()
    Q2.event(5, 6)
    I1.arrive()
    for n, me, rows_of, block in ((Z, y, key_row, key_all), (Y, z, value_row, value_all)):
        shape = (n * cands, n * 16)
        r, c = iota(shape, 0), iota(shape, 1)
        sel = jnp.where(c == lax.div(r, jnp.int32(cands)) * 16 + lax.rem(r, jnp.int32(cands)), 1.0, 0.0)
        block[me] = dot(sel.astype(BF16), rows_of[...].reshape(n * 16, HD)).astype(BF16)
    I2.start()

    qacc[:, :qh] = dot(nrm[...], bqa[...].reshape(TP * width, qh))
    O2.event(0)
    qacc[:, qh:] = dot(nrm[...], bqb[...].reshape(TP * width, qh))
    asked = jnp.zeros((16, HD), F32)
    for j in range(cands):
        for h in range(group):
            qbuf[j, pl.ds(h * SEQ, SEQ)] = norm_rope(
                qacc[pl.ds(j * SEQ, SEQ), pl.ds(h * HD, HD)], q_gain[...]
            )
        shape = (16, group * SEQ)
        h = iota(shape, 0) - group * j
        here = (h >= 0) & (h < group) & (iota(shape, 1) == h * SEQ + positions[j])
        asked += dot(jnp.where(here, 1.0, 0.0).astype(BF16), qbuf[j])
    O2.event(1)

    factor = float(HD) ** (-0.5)
    slot_s, slot_t = iota((SEQ, HD), 0), iota((SEQ, HD), 1)
    for j in range(cands):
        allowed = (slot_t <= slot_s) & (slot_t < lengths[j])
        allowed = jnp.concatenate([allowed.astype(F32)] * group, axis=0) > 0.0
        scores = dot_t(qbuf[j], kbuf[j]) * factor
        e = jnp.where(allowed, jnp.exp(scores), 0.0)
        den = jnp.sum(e, axis=-1, keepdims=True)
        num = dot(e.astype(BF16), vbuf[j])
        here = slot_s == positions[j]
        for h in range(group):
            span = slice(h * SEQ, (h + 1) * SEQ)
            r = group * j + h
            near_den[r : r + 1] = jnp.sum(jnp.where(here, den[span], 0.0), axis=0, keepdims=True)
            near_sum[r : r + 1] = jnp.sum(jnp.where(here, num[span], 0.0), axis=0, keepdims=True)
            mix[t, pl.ds(j * SEQ, SEQ), pl.ds(h * HD, HD)] = (num[span] / den[span]).astype(BF16)
        if j == cands // 2 - 1:
            M.start(0)
    M.start(1)
    O2.event(2)
    O2.event(3)
    steps(M, 0)
    O2.event(4)
    I2.arrive()

    count = Y * Z * cands
    r, c = iota((count, count), 0), iota((count, count), 1)
    inner = lax.rem(r, jnp.int32(cands))
    there = lax.div(r, jnp.int32(cands))
    there = (lax.rem(there, jnp.int32(Y)) * Z + lax.div(there, jnp.int32(Y))) * cands + inner
    order = jnp.where(c == there, 1.0, 0.0).astype(BF16)
    flat = dot(order, key_all[...].reshape(count, HD)).astype(BF16)
    r, c = iota((16, count), 0), iota((16, count), 1)
    there = lax.div(c, jnp.int32(cands))
    there = (lax.rem(there, jnp.int32(Y)) * Z + lax.div(there, jnp.int32(Y))) * cands + lax.rem(
        c, jnp.int32(cands)
    )
    own = cand * cands + lax.div(r, jnp.int32(group))
    far = jnp.where(there != own, jnp.exp(dot_t(asked.astype(BF16), flat) * factor), 0.0)
    den = near_den[...] + jnp.sum(far, axis=-1, keepdims=True)
    num = near_sum[...] + dot(far.astype(BF16), value_all[...].reshape(count, HD))
    mixed = (num / den).astype(BF16)
    row, column = iota((16, 16), 0), iota((16, 16), 1)
    for h in range(group):
        sel = jnp.where((row < cands) & (column == row * group + h), 1.0, 0.0).astype(BF16)
        mix[t, pl.ds(rows, 16), pl.ds(h * HD, HD)] = dot(sel, mixed).astype(BF16)
    T.start()
    steps(M, 1)
    O2.event(5)
    steps(M, 2)
    O2.event(6)
    M.arrive()
    T.arrive()

    total[...] = jnp.zeros_like(total)

    def project(i, carry):
        left = dot_t(mix[i, :, :qh], boa[i].reshape(width, qh))
        total[...] += left + dot_t(mix[i, :, qh:], bob[i].reshape(width, qh))
        return carry

    for n in range(2):
        cols = slice(n * Z // 2, (n + 1) * Z // 2)
        acc = None
        for i in range(TP):
            for k, buf in enumerate((boa, bob)):
                term = dot_t(mix[i, :, k * qh : (k + 1) * qh], buf[i, cols].reshape(width // 2, qh))
                acc = term if acc is None else acc + term
        total[:, n * width // 2 : (n + 1) * width // 2] = acc
    for j in range(cands):
        span = pl.ds(j * SEQ, SEQ)
        here = iota((SEQ, width), 0) == positions[j]
        out[span] = jnp.where(here, total[rows + j : rows + j + 1], total[span]).astype(BF16)

    for chain in (K1, K2, Q1, Q2, O1, O2, I1, I2, H, M, T):
        chain.finish()

    @pl.when(t != y)
    def _():
        for i in range(2):
            swap_copy(i, t).wait_send()


N_SEMS = 256


def shards(
    hidden_in, norm_gain, w_query, w_key, w_value, q_gain, k_gain, w_out, lengths, positions
):
    TP = lax.axis_size("tp")
    Y, Z, X = TP, lax.axis_size("cand") // TP, TP // 2
    rows, width = hidden_in.shape
    depth = w_key.shape[0]
    cands, group = rows // SEQ, w_query.shape[1] // w_key.shape[1]
    qh = group * HD // 2
    cosine, sine = rope_tables()
    any_, vmem, smem = (
        pl.BlockSpec(memory_space=m) for m in (pl.ANY, pltpu.VMEM, pltpu.SMEM)
    )
    return pl.pallas_call(
        functools.partial(kernel, (Y, Z, X, TP, cands, group)),
        out_shape=jax.ShapeDtypeStruct((rows, width), BF16),
        in_specs=[any_, vmem, any_, any_, any_, vmem, vmem, any_, smem, smem, vmem, vmem],
        out_specs=vmem,
        scratch_shapes=[
            pltpu.VMEM((TP, rows, width), BF16),
            pltpu.VMEM((rows, TP * width), BF16),
            pltpu.VMEM((Y, Z, depth, HD), BF16),
            pltpu.VMEM((Y, Z, depth, HD), BF16),
            pltpu.VMEM((Y, Z, depth, qh), BF16),
            pltpu.VMEM((Y, Z, depth, qh), BF16),
            pltpu.VMEM((Y, Z, depth, qh), BF16),
            pltpu.VMEM((Y, Z, depth, qh), BF16),
            pltpu.VMEM((Z, 16, HD), BF16),
            pltpu.VMEM((Y, 16, HD), BF16),
            pltpu.VMEM((Y, Z * cands, HD), BF16),
            pltpu.VMEM((Z, Y * cands, HD), BF16),
            pltpu.VMEM((depth, 2 * qh), BF16),
            pltpu.VMEM((cands, HD, HD), BF16),
            pltpu.VMEM((cands, HD, HD), BF16),
            pltpu.VMEM((rows, 2 * HD), F32),
            pltpu.VMEM((rows, group * HD), F32),
            pltpu.VMEM((cands, group * SEQ, HD), BF16),
            pltpu.VMEM((TP, rows + 16, group * HD), BF16),
            pltpu.VMEM((rows + 16, width), F32),
            pltpu.VMEM((16, HD), F32),
            pltpu.VMEM((16, HD), F32),
            pltpu.SemaphoreType.DMA((N_SEMS,)),
            pltpu.SemaphoreType.DMA((N_SEMS,)),
            pltpu.SemaphoreType.DMA((6,)),
        ],
        compiler_params=pltpu.CompilerParams(
            collective_id=0, has_side_effects=True, vmem_limit_bytes=56 * 1024 * 1024
        ),
        cost_estimate=pl.CostEstimate(flops=4 * 10**9, bytes_accessed=2 * 10**6, transcendentals=10**6),
    )(
        hidden_in,
        norm_gain[None],
        w_query,
        w_key,
        w_value,
        q_gain[None],
        k_gain[None],
        w_out.T,
        lengths,
        positions,
        jnp.asarray(cosine),
        jnp.asarray(sine),
    )


def solution(mesh):
    in_specs = (
        P("cand", "tp"),
        P(),
        P("cand", "tp"),
        P("cand", "tp"),
        P("cand", "tp"),
        P(),
        P(),
        P("tp", "cand"),
        P("cand"),
        P("cand"),
    )
    out_specs = P("cand", "tp")
    return jax.shard_map(shards, mesh=mesh, in_specs=in_specs, out_specs=out_specs, check_vma=False)
```

```python
import functools

import jax
import jax.numpy as jnp
import numpy as np
from jax import lax
from jax.experimental import pallas as pl
from jax.experimental.pallas import tpu as pltpu
from jax.sharding import PartitionSpec as P

HD = 128
SEQ = 96
EPSILON = 1e-06
THETA = 1000000.0
F32, BF16 = jnp.float32, jnp.bfloat16
MESH = pl.DeviceIdType.MESH


def rope_tables():
    half = HD // 2
    frequency = np.float32(THETA) ** (-(np.arange(half, dtype=np.float32) * np.float32(2.0 / HD)))
    angles = np.arange(SEQ, dtype=np.float32)[:, None] * frequency.astype(np.float32)[None, :]
    cosine, sine = np.cos(angles), np.sin(angles)
    return (
        np.concatenate([cosine, cosine], axis=-1).astype(np.float32),
        np.concatenate([-sine, sine], axis=-1).astype(np.float32),
    )


def ring_plan(n, halves):
    far = n // 2
    if n == 1:
        return {1: [], -1: []}
    if halves == 1:
        return {
            1: [(d, 0) for d in range(1, far + 1)],
            -1: [(d, 0) for d in range(1, n - far)],
        }
    return {
        1: [(d, k) for d in range(1, far + 1) for k in (0, 1) if d < far or k == 0],
        -1: [(d, k) for d in range(1, far + 1) for k in (1, 0) if d < far or k == 1],
    }


class Sems:
    def __init__(self, send, recv):
        self.send, self.recv, self.used = send, recv, 0

    def take(self):
        self.used += 1
        return self.used - 1


class Ring:
    def __init__(self, n, me, slot, peer, sems, halves=2):
        self.n, self.me, self.slot, self.peer, self.sems = n, me, slot, peer, sems
        self.plan = ring_plan(n, halves)
        self.ids = {(s, *m): sems.take() for s in (1, -1) for m in self.plan[s]}
        self.rounds = max(len(self.plan[1]), len(self.plan[-1]))
        self.sent = []

    def at(self, offset):
        return lax.rem(self.me + offset + self.n, self.n)

    def copy(self, place, way, dist, half):
        ref, k = self.slot(place, half), self.ids[way, dist, half]
        return pltpu.make_async_remote_copy(
            src_ref=ref,
            dst_ref=ref,
            send_sem=self.sems.send.at[k],
            recv_sem=self.sems.recv.at[k],
            device_id=self.peer(self.at(way)),
            device_id_type=MESH,
        )

    def send(self, way, dist, half):
        copy = self.copy(self.at(-way * (dist - 1)), way, dist, half)
        copy.start()
        self.sent.append(copy)

    def start(self, half=None):
        for k in range(2):
            for way in (1, -1):
                mine = [m for m in self.plan[way] if m[0] == 1]
                if k < len(mine) and half in (None, mine[k][1]):
                    self.send(way, *mine[k])

    def event(self, r):
        got = []
        for way in (1, -1):
            if r < len(self.plan[way]):
                dist, half = self.plan[way][r]
                self.copy(self.at(-way * dist), way, dist, half).wait_recv()
                if (dist + 1, half) in self.plan[way]:
                    self.send(way, dist + 1, half)
                got.append((self.at(-way * dist), half))
        return got

    def finish(self):
        for copy in self.sent:
            copy.wait_send()


class Group:
    def __init__(self, *rings):
        self.rings = rings
        self.rounds = max(getattr(r, "rounds", 0) for r in rings)

    def start(self):
        for ring in self.rings:
            ring.start()

    def event(self, *which):
        for r in which:
            for ring in self.rings:
                ring.event(r)

    def all(self):
        self.event(*range(self.rounds))

    def relay(self):
        for ring in self.rings:
            ring.relay()

    def arrive(self):
        for ring in self.rings:
            ring.arrive()

    def finish(self):
        for ring in self.rings:
            ring.finish()


class Direct:
    def __init__(self, n, me, slot, peer, sems, sign, relay=False):
        self.n, self.me, self.slot, self.peer, self.sems, self.sign = n, me, slot, peer, sems, sign
        self.order = sorted(range(1, n), key=lambda d: (min(d, n - d), d))
        self.ids = {d: sems.take() for d in self.order}
        self.via = {3: (2, 1), 4: (2, 2), 5: (6, 7)} if relay and n == 8 else {}
        self.sent, self.relayed = [], False

    def at(self, dist):
        return lax.rem(self.me + self.sign * dist + self.n, self.n)

    def copy(self, dist, place, hop):
        ref = self.slot(place)
        return pltpu.make_async_remote_copy(
            src_ref=ref,
            dst_ref=ref,
            send_sem=self.sems.send.at[self.ids[dist]],
            recv_sem=self.sems.recv.at[self.ids[dist]],
            device_id=self.peer(self.at(hop)),
            device_id_type=MESH,
        )

    def send(self, dist, place, hop):
        copy = self.copy(dist, place, hop)
        copy.start()
        self.sent.append(copy)

    def take(self, dist):
        self.copy(dist, self.at(-dist), dist).wait_recv()

    def start(self):
        for dist in reversed(self.order):
            if dist not in self.via:
                self.send(dist, self.me, dist)

    def relay(self):
        for first in sorted({f for f, _ in self.via.values()}):
            self.take(first)
            for dist, (source, hop) in self.via.items():
                if source == first:
                    self.send(dist, self.at(-first), hop)
        self.relayed = True

    def arrive(self):
        if not self.relayed:
            self.relay()
        firsts = {f for f, _ in self.via.values()}
        for dist in self.order:
            if dist not in firsts:
                self.take(dist)

    def finish(self):
        for copy in self.sent:
            copy.wait_send()


class ChipGather:
    def __init__(self, n, x, core, cand, buf, rows, sems):
        def slot(i, half):
            return buf.at[i * 2 + core, pl.ds(half * rows, rows)]

        self.ring = Ring(n, x, slot, lambda i: (cand, i * 2 + core), sems)
        self.sems, self.buf, self.rows = sems, buf, rows
        self.n, self.x, self.core = n, x, core
        self.other = (cand, x * 2 + 1 - core)
        self.sent, self.due = [], []

    def pass_on(self, place, half):
        k = self.sems.take()
        mine = self.buf.at[place * 2 + self.core, pl.ds(half * self.rows, self.rows)]
        theirs = self.buf.at[place * 2 + 1 - self.core, pl.ds(half * self.rows, self.rows)]

        def copy(ref):
            return pltpu.make_async_remote_copy(
                src_ref=ref,
                dst_ref=ref,
                send_sem=self.sems.send.at[k],
                recv_sem=self.sems.recv.at[k],
                device_id=self.other,
                device_id_type=MESH,
            )

        out = copy(mine)
        out.start()
        self.sent.append(out)
        self.due.append(copy(theirs))

    def start(self, half=None):
        self.ring.start(half)
        for k in (0, 1):
            if half in (None, k):
                self.pass_on(self.x, k)

    def event(self, *which):
        for r in which:
            for place, half in self.ring.event(r):
                self.pass_on(place, half)

    def arrive(self):
        for copy in self.due:
            copy.wait_recv()

    def finish(self):
        self.ring.finish()
        for copy in self.sent:
            copy.wait_send()


def dot(a, b):
    return jnp.dot(a, b, preferred_element_type=F32)


def dot_t(a, b):
    return lax.dot_general(a, b, (((1,), (1,)), ((), ())), preferred_element_type=F32)


def iota(shape, axis):
    return lax.broadcasted_iota(jnp.int32, shape, axis)


def kernel(
    sizes,
    hidden,
    gain_in,
    w_query,
    w_key,
    w_value,
    q_gain_in,
    k_gain_in,
    w_out,
    lengths_in,
    positions_in,
    cosine_in,
    sine_in,
    out,
    gain,
    q_gain,
    k_gain,
    lengths,
    positions,
    cosine,
    sine,
    hid,
    nrm,
    bk,
    bv,
    bqa,
    bqb,
    boa,
    bob,
    key_row,
    value_row,
    key_all,
    value_all,
    raw,
    kbuf,
    vbuf,
    kacc,
    qacc,
    qbuf,
    mix,
    total,
    near_den,
    near_sum,
    send,
    recv,
    local,
):
    Y, Z, X, TP, cands, group = sizes
    cand, t = lax.axis_index("cand"), lax.axis_index("tp")
    y, z = cand // Z, lax.rem(cand, Z)
    x, core = t // 2, lax.rem(t, 2)
    rows = cands * SEQ
    depth = w_key.shape[0]
    width = hidden.shape[1]
    half = depth // 2
    qh = group * HD // 2
    sems = Sems(send, recv)

    fetches = [
        pltpu.make_async_copy(src, dst, local.at[i])
        for i, (src, dst) in enumerate(
            [
                (w_key, bk.at[y, z]),
                (w_value, bv.at[y, z]),
                (hidden, hid.at[t]),
                (w_query.at[:, pl.ds(0, qh)], bqa.at[y, z]),
                (w_query.at[:, pl.ds(qh, qh)], bqb.at[y, z]),
                (w_out, raw),
                (gain_in, gain),
                (q_gain_in, q_gain),
                (k_gain_in, k_gain),
                (cosine_in, cosine),
                (sine_in, sine),
                (lengths_in, lengths),
                (positions_in, positions),
            ]
        )
    ]
    for fetch in fetches:
        fetch.start()

    def along_y(i):
        return (i * Z + z, t)

    def along_z(i):
        return (y * Z + i, t)

    def along_tp(i):
        return (cand, i)

    barrier = pltpu.get_barrier_semaphore()
    near = []
    for n, me, peer in ((Y, y, along_y), (Z, z, along_z)):
        near += [peer(lax.rem(me + i, n)) for i in range(1, n)]
    near += [along_tp(lax.rem(t + i, TP)) for i in range(1, TP)]
    swap = (t * Z + z, y)
    near.append(swap)
    for peer in near:
        pl.semaphore_signal(barrier, inc=1, device_id=peer, device_id_type=MESH)
    pl.semaphore_wait(barrier, len(near))

    sign = 1 - 2 * core

    def gather(a, b, direct, relay=False):
        def part(k):
            return pl.ds(k * half, half)

        if direct:
            first = Group(
                Direct(Y, y, lambda i: a.at[i, z], along_y, sems, sign, relay),
                Direct(Z, z, lambda i: b.at[y, i], along_z, sems, sign, relay),
            )
        else:
            first = Group(
                Ring(Y, y, lambda i, k: a.at[i, z, part(k)], along_y, sems),
                Ring(Z, z, lambda i, k: b.at[y, i, part(k)], along_z, sems),
            )
        second = Group(
            Ring(Z, z, lambda i, k: a.at[:, i, part(k)], along_z, sems),
            Ring(Y, y, lambda i, k: b.at[i, :, part(k)], along_y, sems),
        )
        return first, second

    K1, K2 = gather(bk, bv, True)
    Q1, Q2 = gather(bqa, bqb, True)
    O1, O2 = gather(boa, bob, False)
    I1 = Group(
        Direct(Z, z, lambda i: key_row.at[i], along_z, sems, sign),
        Direct(Y, y, lambda i: value_row.at[i], along_y, sems, sign),
    )
    I2 = Group(
        Direct(Y, y, lambda i: key_all.at[i], along_y, sems, sign),
        Direct(Z, z, lambda i: value_all.at[i], along_z, sems, sign),
    )
    H = ChipGather(X, x, core, cand, hid, rows // 2, sems)
    T = Direct(TP, t, lambda i: mix.at[i, pl.ds(rows, 16)], along_tp, sems, sign)
    M = ChipGather(X, x, core, cand, mix, rows // 2, sems)

    fetches[0].wait()
    fetches[1].wait()
    K1.start()
    fetches[2].wait()
    H.start()
    fetches[3].wait()
    fetches[4].wait()
    Q1.start()

    fetches[5].wait()
    swaps = [sems.take(), sems.take()]

    def swap_copy(i, place):
        return pltpu.make_async_remote_copy(
            src_ref=raw.at[:, pl.ds(i * qh, qh)],
            dst_ref=(boa, bob)[i].at[place, z],
            send_sem=send.at[swaps[i]],
            recv_sem=recv.at[swaps[i]],
            device_id=swap,
            device_id_type=MESH,
        )

    @pl.when(t != y)
    def _():
        for i in range(2):
            swap_copy(i, t).start()

    @pl.when(t == y)
    def _():
        for i in range(2):
            (boa, bob)[i][y, z] = raw[:, pl.ds(i * qh, qh)]

    def steps(gather, r):
        if r < gather.ring.rounds:
            gather.event(r)

    K1.arrive()
    K2.start()
    steps(H, 0)
    Q1.arrive()
    Q2.start()
    K2.event(0, 1)
    steps(H, 1)
    Q2.event(0)
    K2.event(2, 3)

    @pl.when(t != y)
    def _():
        for i in range(2):
            swap_copy(i, y).wait_recv()

    O1.start()
    Q2.event(1)
    steps(H, 2)
    K2.event(4, 5)
    H.arrive()

    for fetch in fetches[6:]:
        fetch.wait()

    def squares(i, acc):
        v = hid[i].astype(F32)
        return acc + jnp.sum(v * v, axis=-1, keepdims=True)

    square = lax.fori_loop(0, TP, squares, jnp.zeros((rows, 1), F32))
    inverse = lax.rsqrt(square * (1.0 / (TP * width)) + EPSILON)

    def scale(i, carry):
        lanes = pl.ds(pl.multiple_of(i * width, 128), width)
        nrm[:, lanes] = (hid[i].astype(F32) * inverse * gain[:, lanes]).astype(BF16)
        return carry

    Q2.event(2)
    K2.event(6)
    lax.fori_loop(0, TP, scale, 0)
    O1.event(0, 1)

    def norm_rope(v, weight):
        v = v * lax.rsqrt(jnp.mean(v * v, axis=-1, keepdims=True) + EPSILON) * weight
        return (v * cosine[...] + pltpu.roll(v, HD // 2, 1) * sine[...]).astype(BF16)

    kacc[:, :HD] = dot(nrm[...], bk[...].reshape(TP * width, HD))
    kacc[:, HD:] = dot(nrm[...], bv[...].reshape(TP * width, HD))
    Q2.event(3)
    O1.event(2, 3)
    pad = jnp.zeros((HD - SEQ, HD), BF16)
    picked = [jnp.zeros((16, HD), F32)] * 2
    for j in range(cands):
        span = pl.ds(j * SEQ, SEQ)
        kj = norm_rope(kacc[span, :HD], k_gain[...])
        vj = kacc[span, HD:].astype(BF16)
        kbuf[j] = jnp.concatenate([kj, pad], axis=0)
        vbuf[j] = jnp.concatenate([vj, pad], axis=0)
        here = iota((16, HD), 1) == positions[j]
        sel = jnp.where(here & (iota((16, HD), 0) == j), 1.0, 0.0).astype(BF16)
        picked = [p + dot(sel, block[j]) for p, block in zip(picked, (kbuf, vbuf))]
    key_row[z] = picked[0].astype(BF16)
    value_row[y] = picked[1].astype(BF16)
    I1.start()
    Q2.event(4)
    O1.event(4, 5, 6)
    O2.start()
    Q2.event(5, 6)
    I1.arrive()
    for n, me, rows_of, block in ((Z, y, key_row, key_all), (Y, z, value_row, value_all)):
        shape = (n * cands, n * 16)
        r, c = iota(shape, 0), iota(shape, 1)
        sel = jnp.where(c == lax.div(r, jnp.int32(cands)) * 16 + lax.rem(r, jnp.int32(cands)), 1.0, 0.0)
        block[me] = dot(sel.astype(BF16), rows_of[...].reshape(n * 16, HD)).astype(BF16)
    I2.start()

    qacc[:, :qh] = dot(nrm[...], bqa[...].reshape(TP * width, qh))
    qacc[:, qh:] = dot(nrm[...], bqb[...].reshape(TP * width, qh))
    asked = jnp.zeros((16, HD), F32)
    for j in range(cands):
        for h in range(group):
            qbuf[j, pl.ds(h * SEQ, SEQ)] = norm_rope(
                qacc[pl.ds(j * SEQ, SEQ), pl.ds(h * HD, HD)], q_gain[...]
            )
        shape = (16, group * SEQ)
        h = iota(shape, 0) - group * j
        here = (h >= 0) & (h < group) & (iota(shape, 1) == h * SEQ + positions[j])
        asked += dot(jnp.where(here, 1.0, 0.0).astype(BF16), qbuf[j])
    factor = float(HD) ** (-0.5)
    slot_s, slot_t = iota((SEQ, HD), 0), iota((SEQ, HD), 1)
    for j in range(cands):
        allowed = (slot_t <= slot_s) & (slot_t < lengths[j])
        allowed = jnp.concatenate([allowed.astype(F32)] * group, axis=0) > 0.0
        scores = dot_t(qbuf[j], kbuf[j]) * factor
        e = jnp.where(allowed, jnp.exp(scores), 0.0)
        den = jnp.sum(e, axis=-1, keepdims=True)
        num = dot(e.astype(BF16), vbuf[j])
        here = slot_s == positions[j]
        for h in range(group):
            span = slice(h * SEQ, (h + 1) * SEQ)
            r = group * j + h
            near_den[r : r + 1] = jnp.sum(jnp.where(here, den[span], 0.0), axis=0, keepdims=True)
            near_sum[r : r + 1] = jnp.sum(jnp.where(here, num[span], 0.0), axis=0, keepdims=True)
            mix[t, pl.ds(j * SEQ, SEQ), pl.ds(h * HD, HD)] = (num[span] / den[span]).astype(BF16)
        if j == cands // 2 - 1:
            M.start(0)
            O2.event(0)
    M.start(1)
    O2.event(1, 2)
    steps(M, 0)
    O2.event(3)
    I2.arrive()

    count = Y * Z * cands
    r, c = iota((count, count), 0), iota((count, count), 1)
    inner = lax.rem(r, jnp.int32(cands))
    there = lax.div(r, jnp.int32(cands))
    there = (lax.rem(there, jnp.int32(Y)) * Z + lax.div(there, jnp.int32(Y))) * cands + inner
    order = jnp.where(c == there, 1.0, 0.0).astype(BF16)
    flat = dot(order, key_all[...].reshape(count, HD)).astype(BF16)
    r, c = iota((16, count), 0), iota((16, count), 1)
    there = lax.div(c, jnp.int32(cands))
    there = (lax.rem(there, jnp.int32(Y)) * Z + lax.div(there, jnp.int32(Y))) * cands + lax.rem(
        c, jnp.int32(cands)
    )
    own = cand * cands + lax.div(r, jnp.int32(group))
    far = jnp.where(there != own, jnp.exp(dot_t(asked.astype(BF16), flat) * factor), 0.0)
    den = near_den[...] + jnp.sum(far, axis=-1, keepdims=True)
    num = near_sum[...] + dot(far.astype(BF16), value_all[...].reshape(count, HD))
    mixed = (num / den).astype(BF16)
    row, column = iota((16, 16), 0), iota((16, 16), 1)
    for h in range(group):
        sel = jnp.where((row < cands) & (column == row * group + h), 1.0, 0.0).astype(BF16)
        mix[t, pl.ds(rows, 16), pl.ds(h * HD, HD)] = dot(sel, mixed).astype(BF16)
    T.start()
    O2.event(4)
    steps(M, 1)
    O2.event(5)
    steps(M, 2)
    O2.event(6)
    M.arrive()
    T.arrive()

    total[...] = jnp.zeros_like(total)

    def project(i, carry):
        left = dot_t(mix[i, :, :qh], boa[i].reshape(width, qh))
        total[...] += left + dot_t(mix[i, :, qh:], bob[i].reshape(width, qh))
        return carry

    for n in range(2):
        cols = slice(n * Z // 2, (n + 1) * Z // 2)
        acc = None
        for i in range(TP):
            for k, buf in enumerate((boa, bob)):
                term = dot_t(mix[i, :, k * qh : (k + 1) * qh], buf[i, cols].reshape(width // 2, qh))
                acc = term if acc is None else acc + term
        total[:, n * width // 2 : (n + 1) * width // 2] = acc
    for j in range(cands):
        span = pl.ds(j * SEQ, SEQ)
        here = iota((SEQ, width), 0) == positions[j]
        out[span] = jnp.where(here, total[rows + j : rows + j + 1], total[span]).astype(BF16)

    for chain in (K1, K2, Q1, Q2, O1, O2, I1, I2, H, M, T):
        chain.finish()

    @pl.when(t != y)
    def _():
        for i in range(2):
            swap_copy(i, t).wait_send()


N_SEMS = 256


def shards(
    hidden_in, norm_gain, w_query, w_key, w_value, q_gain, k_gain, w_out, lengths, positions
):
    TP = lax.axis_size("tp")
    Y, Z, X = TP, lax.axis_size("cand") // TP, TP // 2
    rows, width = hidden_in.shape
    depth = w_key.shape[0]
    cands, group = rows // SEQ, w_query.shape[1] // w_key.shape[1]
    qh = group * HD // 2
    cosine, sine = rope_tables()
    any_, vmem = (pl.BlockSpec(memory_space=m) for m in (pl.ANY, pltpu.VMEM))
    return pl.pallas_call(
        functools.partial(kernel, (Y, Z, X, TP, cands, group)),
        out_shape=jax.ShapeDtypeStruct((rows, width), BF16),
        in_specs=[any_] * 12,
        out_specs=vmem,
        scratch_shapes=[
            pltpu.VMEM((1, TP * width), F32),
            pltpu.VMEM((1, HD), F32),
            pltpu.VMEM((1, HD), F32),
            pltpu.SMEM(lengths.shape, jnp.int32),
            pltpu.SMEM(positions.shape, jnp.int32),
            pltpu.VMEM((SEQ, HD), F32),
            pltpu.VMEM((SEQ, HD), F32),
            pltpu.VMEM((TP, rows, width), BF16),
            pltpu.VMEM((rows, TP * width), BF16),
            pltpu.VMEM((Y, Z, depth, HD), BF16),
            pltpu.VMEM((Y, Z, depth, HD), BF16),
            pltpu.VMEM((Y, Z, depth, qh), BF16),
            pltpu.VMEM((Y, Z, depth, qh), BF16),
            pltpu.VMEM((Y, Z, depth, qh), BF16),
            pltpu.VMEM((Y, Z, depth, qh), BF16),
            pltpu.VMEM((Z, 16, HD), BF16),
            pltpu.VMEM((Y, 16, HD), BF16),
            pltpu.VMEM((Y, Z * cands, HD), BF16),
            pltpu.VMEM((Z, Y * cands, HD), BF16),
            pltpu.VMEM((depth, 2 * qh), BF16),
            pltpu.VMEM((cands, HD, HD), BF16),
            pltpu.VMEM((cands, HD, HD), BF16),
            pltpu.VMEM((rows, 2 * HD), F32),
            pltpu.VMEM((rows, group * HD), F32),
            pltpu.VMEM((cands, group * SEQ, HD), BF16),
            pltpu.VMEM((TP, rows + 16, group * HD), BF16),
            pltpu.VMEM((rows + 16, width), F32),
            pltpu.VMEM((16, HD), F32),
            pltpu.VMEM((16, HD), F32),
            pltpu.SemaphoreType.DMA((N_SEMS,)),
            pltpu.SemaphoreType.DMA((N_SEMS,)),
            pltpu.SemaphoreType.DMA((13,)),
        ],
        compiler_params=pltpu.CompilerParams(
            collective_id=0, has_side_effects=True, vmem_limit_bytes=56 * 1024 * 1024
        ),
        cost_estimate=pl.CostEstimate(flops=4 * 10**9, bytes_accessed=2 * 10**6, transcendentals=10**6),
    )(
        hidden_in,
        norm_gain[None],
        w_query,
        w_key,
        w_value,
        q_gain[None],
        k_gain[None],
        w_out.T,
        lengths,
        positions,
        jnp.asarray(cosine),
        jnp.asarray(sine),
    )


def solution(mesh):
    in_specs = (
        P("cand", "tp"),
        P(),
        P("cand", "tp"),
        P("cand", "tp"),
        P("cand", "tp"),
        P(),
        P(),
        P("tp", "cand"),
        P("cand"),
        P("cand"),
    )
    out_specs = P("cand", "tp")
    return jax.shard_map(shards, mesh=mesh, in_specs=in_specs, out_specs=out_specs, check_vma=False)
```

```python
import functools

import jax
import jax.numpy as jnp
import numpy as np
from jax import lax
from jax.experimental import pallas as pl
from jax.experimental.pallas import tpu as pltpu
from jax.sharding import PartitionSpec as P

HD = 128
SEQ = 96
EPSILON = 1e-06
THETA = 1000000.0
F32, BF16 = jnp.float32, jnp.bfloat16
MESH = pl.DeviceIdType.MESH


def rope_tables():
    half = HD // 2
    frequency = np.float32(THETA) ** (-(np.arange(half, dtype=np.float32) * np.float32(2.0 / HD)))
    angles = np.arange(SEQ, dtype=np.float32)[:, None] * frequency.astype(np.float32)[None, :]
    cosine, sine = np.cos(angles), np.sin(angles)
    return (
        np.concatenate([cosine, cosine], axis=-1).astype(np.float32),
        np.concatenate([-sine, sine], axis=-1).astype(np.float32),
    )


def ring_plan(n, halves):
    far = n // 2
    if n == 1:
        return {1: [], -1: []}
    if halves == 1:
        return {
            1: [(d, 0) for d in range(1, far + 1)],
            -1: [(d, 0) for d in range(1, n - far)],
        }
    return {
        1: [(d, k) for d in range(1, far + 1) for k in (0, 1) if d < far or k == 0],
        -1: [(d, k) for d in range(1, far + 1) for k in (1, 0) if d < far or k == 1],
    }


class Sems:
    def __init__(self, send, recv):
        self.send, self.recv, self.used = send, recv, 0

    def take(self):
        self.used += 1
        return self.used - 1


class Ring:
    def __init__(self, n, me, slot, peer, sems, halves=2):
        self.n, self.me, self.slot, self.peer, self.sems = n, me, slot, peer, sems
        self.plan = ring_plan(n, halves)
        self.ids = {(s, *m): sems.take() for s in (1, -1) for m in self.plan[s]}
        self.rounds = max(len(self.plan[1]), len(self.plan[-1]))
        self.sent = []

    def at(self, offset):
        return lax.rem(self.me + offset + self.n, self.n)

    def copy(self, place, way, dist, half):
        ref, k = self.slot(place, half), self.ids[way, dist, half]
        return pltpu.make_async_remote_copy(
            src_ref=ref,
            dst_ref=ref,
            send_sem=self.sems.send.at[k],
            recv_sem=self.sems.recv.at[k],
            device_id=self.peer(self.at(way)),
            device_id_type=MESH,
        )

    def send(self, way, dist, half):
        copy = self.copy(self.at(-way * (dist - 1)), way, dist, half)
        copy.start()
        self.sent.append(copy)

    def start(self, half=None):
        for k in range(2):
            for way in (1, -1):
                mine = [m for m in self.plan[way] if m[0] == 1]
                if k < len(mine) and half in (None, mine[k][1]):
                    self.send(way, *mine[k])

    def event(self, r):
        got = []
        for way in (1, -1):
            if r < len(self.plan[way]):
                dist, half = self.plan[way][r]
                self.copy(self.at(-way * dist), way, dist, half).wait_recv()
                if (dist + 1, half) in self.plan[way]:
                    self.send(way, dist + 1, half)
                got.append((self.at(-way * dist), half))
        return got

    def finish(self):
        for copy in self.sent:
            copy.wait_send()


class Group:
    def __init__(self, *rings):
        self.rings = rings
        self.rounds = max(getattr(r, "rounds", 0) for r in rings)

    def start(self):
        for ring in self.rings:
            ring.start()

    def event(self, *which):
        for r in which:
            for ring in self.rings:
                ring.event(r)

    def all(self):
        self.event(*range(self.rounds))

    def relay(self):
        for ring in self.rings:
            ring.relay()

    def arrive(self):
        for ring in self.rings:
            ring.arrive()

    def finish(self):
        for ring in self.rings:
            ring.finish()


class Direct:
    def __init__(self, n, me, slot, peer, sems, sign, relay=False):
        self.n, self.me, self.slot, self.peer, self.sems, self.sign = n, me, slot, peer, sems, sign
        self.order = sorted(range(1, n), key=lambda d: (min(d, n - d), d))
        self.ids = {d: sems.take() for d in self.order}
        self.via = {3: (2, 1), 4: (2, 2), 5: (6, 7)} if relay and n == 8 else {}
        self.sent, self.relayed = [], False

    def at(self, dist):
        return lax.rem(self.me + self.sign * dist + self.n, self.n)

    def copy(self, dist, place, hop):
        ref = self.slot(place)
        return pltpu.make_async_remote_copy(
            src_ref=ref,
            dst_ref=ref,
            send_sem=self.sems.send.at[self.ids[dist]],
            recv_sem=self.sems.recv.at[self.ids[dist]],
            device_id=self.peer(self.at(hop)),
            device_id_type=MESH,
        )

    def send(self, dist, place, hop):
        copy = self.copy(dist, place, hop)
        copy.start()
        self.sent.append(copy)

    def take(self, dist):
        self.copy(dist, self.at(-dist), dist).wait_recv()

    def start(self):
        for dist in reversed(self.order):
            if dist not in self.via:
                self.send(dist, self.me, dist)

    def relay(self):
        for first in sorted({f for f, _ in self.via.values()}):
            self.take(first)
            for dist, (source, hop) in self.via.items():
                if source == first:
                    self.send(dist, self.at(-first), hop)
        self.relayed = True

    def arrive(self):
        if not self.relayed:
            self.relay()
        firsts = {f for f, _ in self.via.values()}
        for dist in self.order:
            if dist not in firsts:
                self.take(dist)

    def finish(self):
        for copy in self.sent:
            copy.wait_send()


class ChipGather:
    def __init__(self, n, x, core, cand, buf, rows, sems):
        def slot(i, half):
            return buf.at[i * 2 + core, pl.ds(half * rows, rows)]

        self.ring = Ring(n, x, slot, lambda i: (cand, i * 2 + core), sems)
        self.sems, self.buf, self.rows = sems, buf, rows
        self.n, self.x, self.core = n, x, core
        self.other = (cand, x * 2 + 1 - core)
        self.sent, self.due = [], []

    def pass_on(self, place, half):
        k = self.sems.take()
        mine = self.buf.at[place * 2 + self.core, pl.ds(half * self.rows, self.rows)]
        theirs = self.buf.at[place * 2 + 1 - self.core, pl.ds(half * self.rows, self.rows)]

        def copy(ref):
            return pltpu.make_async_remote_copy(
                src_ref=ref,
                dst_ref=ref,
                send_sem=self.sems.send.at[k],
                recv_sem=self.sems.recv.at[k],
                device_id=self.other,
                device_id_type=MESH,
            )

        out = copy(mine)
        out.start()
        self.sent.append(out)
        self.due.append(copy(theirs))

    def start(self, half=None):
        self.ring.start(half)
        for k in (0, 1):
            if half in (None, k):
                self.pass_on(self.x, k)

    def event(self, *which):
        for r in which:
            for place, half in self.ring.event(r):
                self.pass_on(place, half)

    def arrive(self):
        for copy in self.due:
            copy.wait_recv()

    def finish(self):
        self.ring.finish()
        for copy in self.sent:
            copy.wait_send()


def dot(a, b):
    return jnp.dot(a, b, preferred_element_type=F32)


def dot_t(a, b):
    return lax.dot_general(a, b, (((1,), (1,)), ((), ())), preferred_element_type=F32)


def iota(shape, axis):
    return lax.broadcasted_iota(jnp.int32, shape, axis)


def kernel(
    sizes,
    hidden,
    gain_in,
    w_query,
    w_key,
    w_value,
    q_gain_in,
    k_gain_in,
    w_out,
    lengths_in,
    positions_in,
    cosine_in,
    sine_in,
    out,
    gain,
    q_gain,
    k_gain,
    lengths,
    positions,
    cosine,
    sine,
    hid,
    nrm,
    bk,
    bv,
    bqa,
    bqb,
    boa,
    bob,
    key_row,
    value_row,
    key_all,
    value_all,
    raw,
    kbuf,
    vbuf,
    kacc,
    qacc,
    qbuf,
    mix,
    total,
    near_den,
    near_sum,
    send,
    recv,
    local,
):
    Y, Z, X, TP, cands, group = sizes
    cand, t = lax.axis_index("cand"), lax.axis_index("tp")
    y, z = cand // Z, lax.rem(cand, Z)
    x, core = t // 2, lax.rem(t, 2)
    rows = cands * SEQ
    depth = w_key.shape[0]
    width = hidden.shape[1]
    half = depth // 2
    qh = group * HD // 2
    sems = Sems(send, recv)

    fetches = [
        pltpu.make_async_copy(src, dst, local.at[i])
        for i, (src, dst) in enumerate(
            [
                (w_key, bk.at[y, z]),
                (w_value, bv.at[y, z]),
                (hidden, hid.at[t]),
                (w_query.at[:, pl.ds(0, qh)], bqa.at[y, z]),
                (w_query.at[:, pl.ds(qh, qh)], bqb.at[y, z]),
                (w_out, raw),
                (gain_in, gain),
                (q_gain_in, q_gain),
                (k_gain_in, k_gain),
                (cosine_in, cosine),
                (sine_in, sine),
                (lengths_in, lengths),
                (positions_in, positions),
            ]
        )
    ]
    for fetch in fetches:
        fetch.start()

    def along_y(i):
        return (i * Z + z, t)

    def along_z(i):
        return (y * Z + i, t)

    def along_tp(i):
        return (cand, i)

    barrier = pltpu.get_barrier_semaphore()
    near = []
    for n, me, peer in ((Y, y, along_y), (Z, z, along_z)):
        near += [peer(lax.rem(me + i, n)) for i in range(1, n)]
    near += [along_tp(lax.rem(t + i, TP)) for i in range(1, TP)]
    swap = (t * Z + z, y)
    near.append(swap)
    for peer in near:
        pl.semaphore_signal(barrier, inc=1, device_id=peer, device_id_type=MESH)
    pl.semaphore_wait(barrier, len(near))

    sign = 1 - 2 * core

    def gather(a, b, direct, relay=False):
        def part(k):
            return pl.ds(k * half, half)

        if direct:
            first = Group(
                Direct(Y, y, lambda i: a.at[i, z], along_y, sems, sign, relay),
                Direct(Z, z, lambda i: b.at[y, i], along_z, sems, sign, relay),
            )
        else:
            first = Group(
                Ring(Y, y, lambda i, k: a.at[i, z, part(k)], along_y, sems),
                Ring(Z, z, lambda i, k: b.at[y, i, part(k)], along_z, sems),
            )
        second = Group(
            Ring(Z, z, lambda i, k: a.at[:, i, part(k)], along_z, sems),
            Ring(Y, y, lambda i, k: b.at[i, :, part(k)], along_y, sems),
        )
        return first, second

    K1, K2 = gather(bk, bv, True)
    Q1, Q2 = gather(bqa, bqb, True)
    O1, O2 = gather(boa, bob, False)
    I1 = Group(
        Direct(Z, z, lambda i: key_row.at[i], along_z, sems, sign),
        Direct(Y, y, lambda i: value_row.at[i], along_y, sems, sign),
    )
    I2 = Group(
        Direct(Y, y, lambda i: key_all.at[i], along_y, sems, sign),
        Direct(Z, z, lambda i: value_all.at[i], along_z, sems, sign),
    )
    H = ChipGather(X, x, core, cand, hid, rows // 2, sems)
    T = Direct(TP, t, lambda i: mix.at[i, pl.ds(rows, 16)], along_tp, sems, sign)
    M = ChipGather(X, x, core, cand, mix, rows // 2, sems)

    fetches[0].wait()
    fetches[1].wait()
    K1.start()
    fetches[3].wait()
    fetches[4].wait()
    Q1.start()
    fetches[2].wait()
    H.start()

    fetches[5].wait()
    swaps = [sems.take(), sems.take()]

    def swap_copy(i, place):
        return pltpu.make_async_remote_copy(
            src_ref=raw.at[:, pl.ds(i * qh, qh)],
            dst_ref=(boa, bob)[i].at[place, z],
            send_sem=send.at[swaps[i]],
            recv_sem=recv.at[swaps[i]],
            device_id=swap,
            device_id_type=MESH,
        )

    @pl.when(t != y)
    def _():
        for i in range(2):
            swap_copy(i, t).start()

    @pl.when(t == y)
    def _():
        for i in range(2):
            (boa, bob)[i][y, z] = raw[:, pl.ds(i * qh, qh)]

    def steps(gather, r):
        if r < gather.ring.rounds:
            gather.event(r)

    K1.arrive()
    K2.start()
    steps(H, 0)
    Q1.arrive()
    Q2.start()
    K2.event(0, 1)
    steps(H, 1)
    Q2.event(0)
    K2.event(2, 3)

    @pl.when(t != y)
    def _():
        for i in range(2):
            swap_copy(i, y).wait_recv()

    O1.start()
    Q2.event(1)
    steps(H, 2)
    K2.event(4, 5)
    H.arrive()

    for fetch in fetches[6:]:
        fetch.wait()

    def squares(i, acc):
        v = hid[i].astype(F32)
        return acc + jnp.sum(v * v, axis=-1, keepdims=True)

    square = lax.fori_loop(0, TP, squares, jnp.zeros((rows, 1), F32))
    inverse = lax.rsqrt(square * (1.0 / (TP * width)) + EPSILON)

    def scale(i, carry):
        lanes = pl.ds(pl.multiple_of(i * width, 128), width)
        nrm[:, lanes] = (hid[i].astype(F32) * inverse * gain[:, lanes]).astype(BF16)
        return carry

    Q2.event(2)
    K2.event(6)
    lax.fori_loop(0, TP, scale, 0)
    O1.event(0, 1)

    def norm_rope(v, weight):
        v = v * lax.rsqrt(jnp.mean(v * v, axis=-1, keepdims=True) + EPSILON) * weight
        return (v * cosine[...] + pltpu.roll(v, HD // 2, 1) * sine[...]).astype(BF16)

    kacc[:, :HD] = dot(nrm[...], bk[...].reshape(TP * width, HD))
    kacc[:, HD:] = dot(nrm[...], bv[...].reshape(TP * width, HD))
    Q2.event(3)
    O1.event(2, 3)
    pad = jnp.zeros((HD - SEQ, HD), BF16)
    picked = [jnp.zeros((16, HD), F32)] * 2
    for j in range(cands):
        span = pl.ds(j * SEQ, SEQ)
        kj = norm_rope(kacc[span, :HD], k_gain[...])
        vj = kacc[span, HD:].astype(BF16)
        kbuf[j] = jnp.concatenate([kj, pad], axis=0)
        vbuf[j] = jnp.concatenate([vj, pad], axis=0)
        here = iota((16, HD), 1) == positions[j]
        sel = jnp.where(here & (iota((16, HD), 0) == j), 1.0, 0.0).astype(BF16)
        picked = [p + dot(sel, block[j]) for p, block in zip(picked, (kbuf, vbuf))]
    key_row[z] = picked[0].astype(BF16)
    value_row[y] = picked[1].astype(BF16)
    I1.start()
    O1.event(4, 5)
    Q2.event(4)
    O1.event(6)
    Q2.event(5)
    O2.start()
    Q2.event(6)
    I1.arrive()
    for n, me, rows_of, block in ((Z, y, key_row, key_all), (Y, z, value_row, value_all)):
        shape = (n * cands, n * 16)
        r, c = iota(shape, 0), iota(shape, 1)
        sel = jnp.where(c == lax.div(r, jnp.int32(cands)) * 16 + lax.rem(r, jnp.int32(cands)), 1.0, 0.0)
        block[me] = dot(sel.astype(BF16), rows_of[...].reshape(n * 16, HD)).astype(BF16)
    I2.start()

    qacc[:, :qh] = dot(nrm[...], bqa[...].reshape(TP * width, qh))
    qacc[:, qh:] = dot(nrm[...], bqb[...].reshape(TP * width, qh))
    asked = jnp.zeros((16, HD), F32)
    for j in range(cands):
        for h in range(group):
            qbuf[j, pl.ds(h * SEQ, SEQ)] = norm_rope(
                qacc[pl.ds(j * SEQ, SEQ), pl.ds(h * HD, HD)], q_gain[...]
            )
        shape = (16, group * SEQ)
        h = iota(shape, 0) - group * j
        here = (h >= 0) & (h < group) & (iota(shape, 1) == h * SEQ + positions[j])
        asked += dot(jnp.where(here, 1.0, 0.0).astype(BF16), qbuf[j])
    factor = float(HD) ** (-0.5)
    slot_s, slot_t = iota((SEQ, HD), 0), iota((SEQ, HD), 1)
    for j in range(cands):
        allowed = (slot_t <= slot_s) & (slot_t < lengths[j])
        allowed = jnp.concatenate([allowed.astype(F32)] * group, axis=0) > 0.0
        scores = dot_t(qbuf[j], kbuf[j]) * factor
        e = jnp.where(allowed, jnp.exp(scores), 0.0)
        den = jnp.sum(e, axis=-1, keepdims=True)
        num = dot(e.astype(BF16), vbuf[j])
        here = slot_s == positions[j]
        for h in range(group):
            span = slice(h * SEQ, (h + 1) * SEQ)
            r = group * j + h
            near_den[r : r + 1] = jnp.sum(jnp.where(here, den[span], 0.0), axis=0, keepdims=True)
            near_sum[r : r + 1] = jnp.sum(jnp.where(here, num[span], 0.0), axis=0, keepdims=True)
            mix[t, pl.ds(j * SEQ, SEQ), pl.ds(h * HD, HD)] = (num[span] / den[span]).astype(BF16)
        if j == cands // 2 - 1:
            M.start(0)
            O2.event(0)
    M.start(1)
    O2.event(1, 2)
    steps(M, 0)
    O2.event(3)
    I2.arrive()

    count = Y * Z * cands
    r, c = iota((count, count), 0), iota((count, count), 1)
    inner = lax.rem(r, jnp.int32(cands))
    there = lax.div(r, jnp.int32(cands))
    there = (lax.rem(there, jnp.int32(Y)) * Z + lax.div(there, jnp.int32(Y))) * cands + inner
    order = jnp.where(c == there, 1.0, 0.0).astype(BF16)
    flat = dot(order, key_all[...].reshape(count, HD)).astype(BF16)
    r, c = iota((16, count), 0), iota((16, count), 1)
    there = lax.div(c, jnp.int32(cands))
    there = (lax.rem(there, jnp.int32(Y)) * Z + lax.div(there, jnp.int32(Y))) * cands + lax.rem(
        c, jnp.int32(cands)
    )
    own = cand * cands + lax.div(r, jnp.int32(group))
    far = jnp.where(there != own, jnp.exp(dot_t(asked.astype(BF16), flat) * factor), 0.0)
    den = near_den[...] + jnp.sum(far, axis=-1, keepdims=True)
    num = near_sum[...] + dot(far.astype(BF16), value_all[...].reshape(count, HD))
    mixed = (num / den).astype(BF16)
    row, column = iota((16, 16), 0), iota((16, 16), 1)
    for h in range(group):
        sel = jnp.where((row < cands) & (column == row * group + h), 1.0, 0.0).astype(BF16)
        mix[t, pl.ds(rows, 16), pl.ds(h * HD, HD)] = dot(sel, mixed).astype(BF16)
    T.start()
    O2.event(4)
    steps(M, 1)
    O2.event(5)
    steps(M, 2)
    O2.event(6)
    M.arrive()
    T.arrive()

    total[...] = jnp.zeros_like(total)

    def project(i, carry):
        left = dot_t(mix[i, :, :qh], boa[i].reshape(width, qh))
        total[...] += left + dot_t(mix[i, :, qh:], bob[i].reshape(width, qh))
        return carry

    for n in range(2):
        cols = slice(n * Z // 2, (n + 1) * Z // 2)
        acc = None
        for i in range(TP):
            for k, buf in enumerate((boa, bob)):
                term = dot_t(mix[i, :, k * qh : (k + 1) * qh], buf[i, cols].reshape(width // 2, qh))
                acc = term if acc is None else acc + term
        total[:, n * width // 2 : (n + 1) * width // 2] = acc
    for j in range(cands):
        span = pl.ds(j * SEQ, SEQ)
        here = iota((SEQ, width), 0) == positions[j]
        out[span] = jnp.where(here, total[rows + j : rows + j + 1], total[span]).astype(BF16)

    for chain in (K1, K2, Q1, Q2, O1, O2, I1, I2, H, M, T):
        chain.finish()

    @pl.when(t != y)
    def _():
        for i in range(2):
            swap_copy(i, t).wait_send()


N_SEMS = 256


def shards(
    hidden_in, norm_gain, w_query, w_key, w_value, q_gain, k_gain, w_out, lengths, positions
):
    TP = lax.axis_size("tp")
    Y, Z, X = TP, lax.axis_size("cand") // TP, TP // 2
    rows, width = hidden_in.shape
    depth = w_key.shape[0]
    cands, group = rows // SEQ, w_query.shape[1] // w_key.shape[1]
    qh = group * HD // 2
    cosine, sine = rope_tables()
    any_, vmem = (pl.BlockSpec(memory_space=m) for m in (pl.ANY, pltpu.VMEM))
    return pl.pallas_call(
        functools.partial(kernel, (Y, Z, X, TP, cands, group)),
        out_shape=jax.ShapeDtypeStruct((rows, width), BF16),
        in_specs=[any_] * 12,
        out_specs=vmem,
        scratch_shapes=[
            pltpu.VMEM((1, TP * width), F32),
            pltpu.VMEM((1, HD), F32),
            pltpu.VMEM((1, HD), F32),
            pltpu.SMEM(lengths.shape, jnp.int32),
            pltpu.SMEM(positions.shape, jnp.int32),
            pltpu.VMEM((SEQ, HD), F32),
            pltpu.VMEM((SEQ, HD), F32),
            pltpu.VMEM((TP, rows, width), BF16),
            pltpu.VMEM((rows, TP * width), BF16),
            pltpu.VMEM((Y, Z, depth, HD), BF16),
            pltpu.VMEM((Y, Z, depth, HD), BF16),
            pltpu.VMEM((Y, Z, depth, qh), BF16),
            pltpu.VMEM((Y, Z, depth, qh), BF16),
            pltpu.VMEM((Y, Z, depth, qh), BF16),
            pltpu.VMEM((Y, Z, depth, qh), BF16),
            pltpu.VMEM((Z, 16, HD), BF16),
            pltpu.VMEM((Y, 16, HD), BF16),
            pltpu.VMEM((Y, Z * cands, HD), BF16),
            pltpu.VMEM((Z, Y * cands, HD), BF16),
            pltpu.VMEM((depth, 2 * qh), BF16),
            pltpu.VMEM((cands, HD, HD), BF16),
            pltpu.VMEM((cands, HD, HD), BF16),
            pltpu.VMEM((rows, 2 * HD), F32),
            pltpu.VMEM((rows, group * HD), F32),
            pltpu.VMEM((cands, group * SEQ, HD), BF16),
            pltpu.VMEM((TP, rows + 16, group * HD), BF16),
            pltpu.VMEM((rows + 16, width), F32),
            pltpu.VMEM((16, HD), F32),
            pltpu.VMEM((16, HD), F32),
            pltpu.SemaphoreType.DMA((N_SEMS,)),
            pltpu.SemaphoreType.DMA((N_SEMS,)),
            pltpu.SemaphoreType.DMA((13,)),
        ],
        compiler_params=pltpu.CompilerParams(
            collective_id=0, has_side_effects=True, vmem_limit_bytes=56 * 1024 * 1024
        ),
        cost_estimate=pl.CostEstimate(flops=4 * 10**9, bytes_accessed=2 * 10**6, transcendentals=10**6),
    )(
        hidden_in,
        norm_gain[None],
        w_query,
        w_key,
        w_value,
        q_gain[None],
        k_gain[None],
        w_out.T,
        lengths,
        positions,
        jnp.asarray(cosine),
        jnp.asarray(sine),
    )


def solution(mesh):
    in_specs = (
        P("cand", "tp"),
        P(),
        P("cand", "tp"),
        P("cand", "tp"),
        P("cand", "tp"),
        P(),
        P(),
        P("tp", "cand"),
        P("cand"),
        P("cand"),
    )
    out_specs = P("cand", "tp")
    return jax.shard_map(shards, mesh=mesh, in_specs=in_specs, out_specs=out_specs, check_vma=False)
```
